32 devices in a mesh: tile: 32 (over z, y, x, core).
Axes of the slice: x: 2, y: 2, z: 4, core: 2. Of those that a mesh axis runs over, the one named last changes fastest.
Arguments:
- air_state: float32 [8, 256, 128], P(None, 'tile'), may hold values from -6 to 6
- sea_state: float32 [48, 64, 512], P(None, 'tile'), may hold values from -6 to 6
- flux_start: float32 [4, 256, 128], P(None, 'tile'), may hold values from -6 to 6
- air_cells: int32 [32, 5, 1024], P('tile'), may hold values from 0 to 1023
- sea_cells: int32 [32, 5, 1024], P('tile'), may hold values from 0 to 1023
- slot_counts: int32 [32, 5], P('tile'), may hold values from 0 to 1024, as said below
- sea_share: float32 [32, 5, 1024], P('tile'), may hold values from 0.2 to 1
- air_share: float32 [32, 5, 1024], P('tile'), may hold values from 0.2 to 1
- polar_fold_partner: int32 [512], replicated, may hold values from 0 to 511, each once
- wet_mask: int32 [64, 512], P('tile'), may hold values 0 or 1
- air_cotangent: float32 [8, 256, 128], P(None, 'tile'), may hold values from -6 to 6
- sea_cotangent: float32 [48, 64, 512], P(None, 'tile'), may hold values from -6 to 6
- air_encoder: bfloat16 [64, 81], replicated, may hold values from -0.625 to 0.625
- air_depthwise: bfloat16 [64, 9], replicated, may hold values from -2 to 2
- air_expand: bfloat16 [256, 64], replicated, may hold values from -0.75 to 0.75
- air_contract: bfloat16 [64, 256], replicated, may hold values from -0.375 to 0.375
- air_decoder: bfloat16 [12, 64], replicated, may hold values from -0.75 to 0.75
- sea_encoder: bfloat16 [64, 468], replicated, may hold values from -0.25 to 0.25
- sea_depthwise: bfloat16 [64, 9], replicated, may hold values from -2 to 2
- sea_expand: bfloat16 [256, 64], replicated, may hold values from -0.75 to 0.75
- sea_contract: bfloat16 [64, 256], replicated, may hold values from -0.375 to 0.375
- sea_decoder: bfloat16 [48, 64], replicated, may hold values from -0.75 to 0.75
Outputs:
- air_final: float32 [8, 256, 128], P(None, 'tile')
- sea_final: float32 [48, 64, 512], P(None, 'tile')
- air_grad: float32 [8, 256, 128], P(None, 'tile')
- sea_grad: float32 [48, 64, 512], P(None, 'tile')
- flux_grad: float32 [4, 256, 128], P(None, 'tile')
- air_encoder_grad: float32 [64, 81], replicated
- air_depthwise_grad: float32 [64, 9], replicated
- air_expand_grad: float32 [256, 64], replicated
- air_contract_grad: float32 [64, 256], replicated
- air_decoder_grad: float32 [12, 64], replicated
- sea_encoder_grad: float32 [64, 468], replicated
- sea_depthwise_grad: float32 [64, 9], replicated
- sea_expand_grad: float32 [256, 64], replicated
- sea_contract_grad: float32 [64, 256], replicated
- sea_decoder_grad: float32 [48, 64], replicated
The draws below stay inside these ranges and needn't reach their ends.
Inputs may be any that keep to these rules, and one draw needn't show every extreme that they name: `slot_counts`: the number of used slots of each block, from its first slot on; 0 exactly for blocks whose atmosphere band lies off the grid, at least 256 for all others; in every draw some ocean band has 1024 used slots in every block with an atmosphere band on the grid, and some atmosphere band has 1024 used slots with every ocean band that it is paired with. `air_cells`: a cell of atmosphere band a, numbered row * 128 + column within the band. `sea_cells`: a cell of ocean band o, numbered row * 512 + column within the band. `polar_fold_partner`: each column appears once. `wet_mask`: 1 at ocean cells, 0 on land.
All inputs are finite; a program needn't handle non-finite values. No bound on the sum of `wet_mask` on one device may be relied on, other than what follows from the above.
Results may differ from the reference program's by a relative error of at most 0.025.
Values may be sent and summed in bfloat16 or wider, within the bound.
No kernel may reach another device: no remote copies, remote signals or barrier semaphores. Data moves between devices by JAX's collectives and lax.ppermute only.
A program may use at most 128 MiB of HBM per device.

```python
import math
import jax
import jax.numpy as jnp
from jax import lax

C = 64
HID = 256
ACH = 8
NF = 4
STEPS = 2
NEAR = 5
AIR_LONGITUDES = 128
OCOL = 512
SLOTS = 1024
OCH = 48
AIRSTRIP_SITES = 1024
OCELLS = 1024
AIR_LATITUDES = 256
ONROWS = 64
N_TILE = 32


def draw_slot_counts(key, part):
    first_key, second_key, third_key = jax.random.split(jax.random.fold_in(key, 17), 3)
    lowest = max(1, SLOTS // 4)
    counts = jax.random.randint(first_key, (N_TILE, NEAR), lowest, SLOTS + 1)
    full_ocean = jax.random.randint(second_key, (), 0, N_TILE)
    full_air = jax.random.randint(third_key, (), 0, N_TILE)
    bands = jnp.arange(N_TILE)
    partner_band = bands[:, None] + jnp.arange(NEAR)[None, :] - (NEAR - 1) // 2
    counts = jnp.where(bands[:, None] == full_ocean, SLOTS, counts)
    counts = jnp.where(partner_band == full_air, SLOTS, counts)
    inside = (partner_band >= 0) & (partner_band < N_TILE)
    counts = jnp.where(inside, counts, 0)
    return counts.astype(jnp.int32)


def place_ends(result, key, least, largest):
    index_at = [jax.random.randint(jax.random.fold_in(key, axis), (), 0, length) for axis, length in enumerate(result.shape)]
    longest = result.shape.index(max(result.shape))
    beside = index_at[:longest] + [(index_at[longest] + 1) % result.shape[longest]] + index_at[longest + 1:]
    return result.at[tuple(index_at)].set(least).at[tuple(beside)].set(largest)


def block_scale(rng, extent, cuts, smallest, top_value):
    factor_of = 1.0
    for position, parts in cuts:
        steps = jax.random.uniform(jax.random.fold_in(jax.random.fold_in(rng, 6), position), (parts,), jnp.float32, smallest / len(cuts), top_value / len(cuts))
        factor_of = factor_of * jnp.repeat(jnp.exp(steps), extent[position] // parts).reshape((-1,) + (1,) * (len(extent) - 1 - position))
    return factor_of


def bell_draw(stream_key, dims, deviation, most, cuts=(), held_as=jnp.bfloat16):
    drawn = deviation * jax.random.normal(stream_key, dims, jnp.float32)
    if cuts:
        drawn = drawn * block_scale(stream_key, dims, cuts, -0.22, 0.18)
    return jnp.clip(drawn, -most, most).astype(held_as)


def setup_inputs(seed: int = 0) -> dict:
    key_of = jax.random.split(jax.random.key(seed), 23)
    return {
        "air_state": bell_draw(key_of[0], (ACH, AIR_LATITUDES, AIR_LONGITUDES), 1.0, 6.0, ((1, 32),), jnp.float32),
        "sea_state": bell_draw(key_of[1], (OCH, ONROWS, OCOL), 1.0, 6.0, ((1, 32),), jnp.float32),
        "flux_start": bell_draw(key_of[2], (NF, AIR_LATITUDES, AIR_LONGITUDES), 1.0, 6.0, ((1, 32),), jnp.float32),
        "air_cells": place_ends(jax.random.randint(key_of[3], (N_TILE, NEAR, SLOTS), 0, AIRSTRIP_SITES), jax.random.fold_in(key_of[3], 1), 0, AIRSTRIP_SITES - 1).astype(jnp.int32),
        "sea_cells": place_ends(jax.random.randint(key_of[4], (N_TILE, NEAR, SLOTS), 0, OCELLS), jax.random.fold_in(key_of[4], 1), 0, OCELLS - 1).astype(jnp.int32),
        "slot_counts": draw_slot_counts(jax.random.fold_in(key_of[22], 71), 0),
        "sea_share": jnp.clip(0.2 + 0.8 * jax.random.uniform(key_of[6], (N_TILE, NEAR, SLOTS), jnp.float32) ** block_scale(key_of[6], (N_TILE, NEAR, SLOTS), ((0, 32),), -0.2, 0.2), 0.2, 1.0),
        "air_share": jnp.clip(0.2 + 0.8 * jax.random.uniform(key_of[7], (N_TILE, NEAR, SLOTS), jnp.float32) ** block_scale(key_of[7], (N_TILE, NEAR, SLOTS), ((0, 32),), -0.2, 0.2), 0.2, 1.0),
        "polar_fold_partner": jax.random.permutation(key_of[8], OCOL).astype(jnp.int32),
        "wet_mask": place_ends((jax.random.randint(key_of[9], (ONROWS, OCOL), 0, 3) < 2).astype(jnp.int32), jax.random.fold_in(key_of[9], 1), 0, 1),
        "air_cotangent": bell_draw(key_of[10], (ACH, AIR_LATITUDES, AIR_LONGITUDES), 1.0, 6.0, ((1, 32),), jnp.float32),
        "sea_cotangent": bell_draw(key_of[11], (OCH, ONROWS, OCOL), 1.0, 6.0, ((1, 32),), jnp.float32),
        "air_encoder": bell_draw(key_of[12], (C, 9 * (ACH + 1)), (9 * (ACH + 1)) ** -0.5, 0.625),
        "air_depthwise": bell_draw(key_of[13], (C, 9), 9 ** -0.5, 2.0),
        "air_expand": bell_draw(key_of[14], (HID, C), C ** -0.5, 0.75),
        "air_contract": bell_draw(key_of[15], (C, HID), HID ** -0.5, 0.375),
        "air_decoder": bell_draw(key_of[16], (ACH + NF, C), C ** -0.5, 0.75),
        "sea_encoder": bell_draw(key_of[17], (C, 9 * (OCH + NF)), (9 * (OCH + NF)) ** -0.5, 0.25),
        "sea_depthwise": bell_draw(key_of[18], (C, 9), 9 ** -0.5, 2.0),
        "sea_expand": bell_draw(key_of[19], (HID, C), C ** -0.5, 0.75),
        "sea_contract": bell_draw(key_of[20], (C, HID), HID ** -0.5, 0.375),
        "sea_decoder": bell_draw(key_of[21], (OCH, C), C ** -0.5, 0.75),
    }


def taps(extended):
    rows = extended.shape[1] - 2
    pieces = []
    for shift_row in range(3):
        part = extended[:, shift_row:shift_row + rows]
        for shift_col in (-1, 0, 1):
            pieces.append(jnp.roll(part, -shift_col, axis=2))
    return pieces

def encode(encoder, extended):
    stacked = jnp.concatenate(taps(extended), axis=0)
    inputs, rows, width = stacked.shape
    product = jnp.dot(encoder.astype(jnp.bfloat16), stacked.reshape(inputs, rows * width), preferred_element_type=jnp.float32)
    return product.astype(jnp.bfloat16).reshape(-1, rows, width)

def block(params, padded):
    depthwise, expand, contract, decoder = params
    pieces = taps(padded)
    mixed = pieces[0] * depthwise[:, 0][:, None, None]
    for tap in range(1, 9):
        mixed = mixed + pieces[tap] * depthwise[:, tap][:, None, None]
    channels, rows, width = mixed.shape
    flat = mixed.reshape(channels, rows * width)
    centred = flat - lax.optimization_barrier(jnp.mean(flat, axis=0, keepdims=True))
    normed = centred * lax.rsqrt(lax.optimization_barrier(jnp.mean(centred * centred, axis=0, keepdims=True)) + 1e-06)
    hidden = jax.nn.gelu(jnp.dot(expand.astype(jnp.bfloat16), normed.astype(jnp.bfloat16), preferred_element_type=jnp.float32), approximate=True).astype(jnp.bfloat16)
    residual = padded[:, 1:-1].reshape(channels, rows * width) + jnp.dot(contract.astype(jnp.bfloat16), hidden, preferred_element_type=jnp.float32)
    output = jnp.dot(decoder.astype(jnp.bfloat16), residual.astype(jnp.bfloat16), preferred_element_type=jnp.float32)
    return output.reshape(-1, rows, width)

def band_model(weights, extended, first, last, folded, partner):
    features = encode(weights[0], extended).astype(jnp.float32)
    features = features.at[:, 0].set(jnp.where(first, 0.0, features[:, 0]))
    if folded:
        top = features[:, -2][:, partner]
    else:
        top = jnp.zeros_like(features[:, -1])
    features = features.at[:, -1].set(jnp.where(last, top, features[:, -1]))
    return block(weights[1:], features)

def run_joined_climate(weights, field, folded, partner):
    lowered = field.astype(jnp.bfloat16)
    inputs, total, width = lowered.shape
    if folded:
        top = jnp.stack([lowered[:, total - 1][:, partner], lowered[:, total - 2][:, partner]], axis=1)
    else:
        top = jnp.zeros((inputs, 2, width), lowered.dtype)
    padded = jnp.concatenate([jnp.zeros((inputs, 2, width), lowered.dtype), lowered, top], axis=1)
    rows = total // N_TILE

    def one_band(band):
        extended = lax.dynamic_slice_in_dim(padded, band * rows, rows + 4, 1)
        return band_model(weights, extended, band == 0, band == N_TILE - 1, folded, partner)
    bands = lax.map(jax.checkpoint(one_band), jnp.arange(N_TILE, dtype=jnp.int32))
    return jnp.transpose(bands, (1, 0, 2, 3)).reshape(bands.shape[1], total, width)

def reference(air_state, sea_state, flux_start, air_cells, sea_cells, slot_counts, sea_share, air_share, polar_fold_partner, wet_mask, air_cotangent, sea_cotangent, air_encoder, air_depthwise, air_expand, air_contract, air_decoder, sea_encoder, sea_depthwise, sea_expand, sea_contract, sea_decoder):
    bands = jnp.arange(N_TILE, dtype=jnp.int32)
    blocks = jnp.arange(NEAR, dtype=jnp.int32)
    partner_band = jnp.clip(bands[:, None] + blocks[None, :] - (NEAR - 1) // 2, 0, N_TILE - 1).astype(jnp.int32)
    air_for_block = air_cells[partner_band, blocks[None, :], :]
    air_global_mesh = (partner_band[:, :, None] * AIRSTRIP_SITES + air_for_block).reshape(-1)
    marine_global_mesh = (bands[:, None, None] * OCELLS + sea_cells).reshape(-1)
    used = (jnp.arange(SLOTS, dtype=jnp.int32)[None, None, :] < slot_counts[:, :, None]).astype(jnp.float32)
    interpolate_to_sky = (air_share * used).reshape(-1)
    toward_sea = (sea_share * used).reshape(-1)
    wet = wet_mask.astype(jnp.float32)

    def rollout(air_present_state, sea_now, flux_now, air_learned_tensors, sea_params):
        for step in range(STEPS):
            interface_transfer_map = sea_now[0].reshape(-1)
            skin_heat_level = jnp.zeros((N_TILE * AIRSTRIP_SITES,), jnp.float32).at[air_global_mesh].add(interpolate_to_sky * interface_transfer_map[marine_global_mesh])
            flux_flat = flux_now.reshape(NF, -1)
            inbound_energy_map = jnp.zeros((NF, N_TILE * OCELLS), jnp.float32).at[:, marine_global_mesh].add(toward_sea[None] * flux_flat[:, air_global_mesh])
            air_result_state = run_joined_climate(air_learned_tensors, jnp.concatenate([air_present_state, skin_heat_level.reshape(1, AIR_LATITUDES, AIR_LONGITUDES)], axis=0), False, polar_fold_partner)
            sea_out = run_joined_climate(sea_params, jnp.concatenate([sea_now, inbound_energy_map.reshape(NF, ONROWS, OCOL)], axis=0), True, polar_fold_partner)
            flux_now = air_result_state[ACH:]
            air_present_state = air_present_state + air_result_state[:ACH]
            sea_now = sea_now + wet[None] * sea_out
        return (air_present_state, sea_now)
    air_learned_tensors = tuple((weight.astype(jnp.float32) for weight in (air_encoder, air_depthwise, air_expand, air_contract, air_decoder)))
    sea_params = tuple((weight.astype(jnp.float32) for weight in (sea_encoder, sea_depthwise, sea_expand, sea_contract, sea_decoder)))
    finals, pullback = jax.vjp(rollout, air_state, sea_state, flux_start, air_learned_tensors, sea_params)
    air_grad, sea_grad, flux_grad, air_grads, sea_grads = pullback((air_cotangent, sea_cotangent))
    air_scale = 1.0 / math.sqrt(AIR_LATITUDES * AIR_LONGITUDES)
    sea_scale = 1.0 / math.sqrt(ONROWS * OCOL)
    return (finals[0], finals[1], air_grad, sea_grad, flux_grad, air_grads[0] * air_scale, air_grads[1] * air_scale, air_grads[2] * air_scale, air_grads[3] * air_scale, air_grads[4] * air_scale, sea_grads[0] * sea_scale, sea_grads[1] * sea_scale, sea_grads[2] * sea_scale, sea_grads[3] * sea_scale, sea_grads[4] * sea_scale)
```

```python
import math

import jax
import jax.numpy as jnp
import numpy as np
from jax import lax
from jax.experimental import pallas as pl
from jax.experimental.pallas import tpu as pltpu
from jax.sharding import PartitionSpec as P

F32 = jnp.float32
BF = jnp.bfloat16
OFFS = (-2, -1, 0, 1, 2)
LANE = 128
FORWARD_CHUNK, REPLAY_CHUNK, BACKWARD_CHUNK = 1024, 1024, 1024
VMEM_LIMIT = 16 * 1024 * 1024
SURFACE = 4
CHANNELS = 5


def dot(a, b):
    return lax.dot_general(a, b, (((1,), (0,)), ((), ())), preferred_element_type=F32)


def dot_nt(a, b):
    return lax.dot_general(a, b, (((1,), (1,)), ((), ())), preferred_element_type=F32)


def dot_tn(a, b):
    return lax.dot_general(a, b, (((0,), (0,)), ((), ())), preferred_element_type=F32)


def bf(x):
    return x.astype(BF)


def rounded(x):
    return x.astype(BF).astype(F32)


def iota(shape, axis):
    return lax.broadcasted_iota(jnp.int32, shape, axis)


def load_rows(ref):
    return jnp.concatenate([ref[:, r, :] for r in range(ref.shape[1])], axis=1)


def store_rows(ref, x):
    width = ref.shape[2]
    for r in range(ref.shape[1]):
        ref[:, r, :] = x[:, r * width : (r + 1) * width]


def rolled(x, width, by):
    if by == 0:
        return x
    rows = x.shape[1] // width
    return jnp.concatenate(
        [pltpu.roll(x[:, r * width : (r + 1) * width], (-by) % width, 1) for r in range(rows)], axis=1
    )


def onehot(low):
    return jnp.where(bf(iota((LANE, 1), 0)) == bf(low), jnp.ones((), BF), jnp.zeros((), BF))


def to_table(raw):
    pieces = []
    for ch in range(CHANNELS):
        pieces += [raw[ch : ch + 1, LANE * h : LANE * (h + 1)] for h in range(8)]
    return jnp.concatenate(pieces, axis=0)


def from_table(table):
    rows = []
    for ch in range(table.shape[0] // 8):
        rows.append(jnp.concatenate([table[8 * ch + h : 8 * ch + h + 1] for h in range(8)], axis=1))
    return jnp.concatenate(rows, axis=0) if len(rows) > 1 else rows[0]


def moved(table, path):
    from_hi, from_lo, to_hi, to_lo, weight = path
    gathered = dot(bf(table), onehot(from_lo))
    rows = iota((8, 1), 0).astype(F32)
    picks, puts = rows == from_hi, rows == to_hi
    spread = []
    for g in range(0, table.shape[0], 8):
        value = jnp.sum(jnp.where(picks, gathered[g : g + 8], 0.0), axis=0, keepdims=True) * weight
        spread.append(jnp.where(puts, value, 0.0))
    return dot_nt(bf(jnp.concatenate(spread, axis=0)), onehot(to_lo))


def full_paths(rows, forward):
    line = lambda i: rows[i : i + 1]
    base = 8 if forward else 10
    air = [line(i) for i in range(4)] + [line(base) + line(base + 1)]
    sea = [line(i) for i in range(4, 8)] + [line(base + 4) + line(base + 5)]
    return air, sea


def regrid(paths, tables, forward):
    at_air = at_sea = None
    for (to_air, to_sea), table in zip(paths, tables):
        surface, fluxes = table[8 * SURFACE :], table[: 8 * SURFACE]
        first, second = (surface, fluxes) if forward else (fluxes, surface)
        air = moved(first, to_air)
        sea = moved(second, to_sea)
        at_air = air if at_air is None else at_air + air
        at_sea = sea if at_sea is None else at_sea + sea
    return from_table(at_air), from_table(at_sea)


def own_paths(lists_ref, forward):
    lists = lists_ref[...].astype(F32)
    return [full_paths(lists[16 * d : 16 * d + 16], forward) for d in range(len(OFFS))]


def tables_around(flags_ref, own, near, at_a, at_b):
    own, near, at_a, at_b = [ref[...].astype(F32) for ref in (own, near, at_a, at_b)]
    odd, odd_chip = flags_ref[2] > 0, flags_ref[3] > 0
    up, dn = jnp.where(odd_chip, at_b, at_a), jnp.where(odd_chip, at_a, at_b)
    above = jnp.where(odd, up[48:88], near[0:40])
    below = jnp.where(odd, near[0:40], dn[48:88])
    return [up[0:40], above, own[0:40], below, dn[0:40]]


def couple(paths, tables):
    at_air, at_sea = regrid(paths, tables, True)
    return jnp.concatenate([at_sea, at_air, jnp.zeros((3, at_air.shape[1]), F32)], axis=0)


def sides(near, far, odd):
    return jnp.where(odd, far, near), jnp.where(odd, near, far)


def fold_matrix(partner_ref):
    columns = partner_ref.shape[1]
    return bf(jnp.where(iota((columns, columns), 0) == partner_ref[...], 1.0, 0.0))


def features_of(x, enc_ref, width, flags_ref, fold):
    rows = x.shape[1] // width - 4
    if fold is not None:
        top = x[:, (rows + 1) * width : (rows + 2) * width]
        above = x[:, (rows + 2) * width : (rows + 3) * width]
        above = jnp.where(flags_ref[1] > 0, dot(bf(top), fold), above)
        x = jnp.concatenate([x[:, : (rows + 2) * width], above, x[:, (rows + 3) * width :]], axis=1)
    stack = jnp.concatenate([bf(rolled(x, width, by)) for by in (-1, 0, 1)], axis=0)
    span = (rows + 2) * width
    feat = dot(enc_ref[0], stack[:, 0:span])
    for i in (1, 2):
        feat = feat + dot(enc_ref[i], stack[:, i * width : i * width + span])
    feat = rounded(feat)
    below = jnp.where(flags_ref[0] > 0, 0.0, feat[:, :width])
    above = feat[:, (rows + 1) * width :]
    if fold is not None:
        over = dot(bf(feat[:, rows * width : (rows + 1) * width]), fold)
    else:
        over = 0.0
    above = jnp.where(flags_ref[1] > 0, over, above)
    return stack, jnp.concatenate([below, feat[:, width : (rows + 1) * width], above], axis=1)


def mix(feat, dw_ref, width):
    rows = feat.shape[1] // width - 2
    span = rows * width
    shifted = [rolled(feat, width, by) for by in (-1, 0, 1)]
    total = None
    for i in range(3):
        for j in range(3):
            term = shifted[j][:, i * width : i * width + span] * dw_ref[:, 3 * i + j : 3 * i + j + 1]
            total = term if total is None else total + term
    return total, shifted


def normalise(mixed):
    centred = mixed - jnp.mean(mixed, axis=0, keepdims=True)
    inverse = lax.rsqrt(jnp.mean(centred * centred, axis=0, keepdims=True) + 1e-06)
    return centred * inverse, inverse


GELU_A = math.sqrt(2.0 / math.pi)
GELU_B = 0.044715


def gelu_parts(v):
    square = v * v
    tanh = jnp.tanh(GELU_A * v * (1.0 + GELU_B * square))
    half = 0.5 * (1.0 + tanh)
    return v * half, square, tanh, half


def block_forward(mixed, centre, expand, contract, decoder):
    outs = []
    for c in range(0, mixed.shape[1], FORWARD_CHUNK):
        normed, _ = normalise(mixed[:, c : c + FORWARD_CHUNK])
        hidden = gelu_parts(dot(expand, bf(normed)))[0]
        residual = centre[:, c : c + FORWARD_CHUNK] + dot(contract, bf(hidden))
        outs.append(dot(decoder, bf(residual)))
    return jnp.concatenate(outs, axis=1)


def block_replay(mixed, centre, expand, contract, keep):
    normed_ref, inverse_ref, hid_ref, slope_ref, residual_ref = keep
    for c in range(0, mixed.shape[1], REPLAY_CHUNK):
        at = slice(c, c + REPLAY_CHUNK)
        normed, inverse = normalise(mixed[:, at])
        pre = dot(expand, bf(normed))
        hidden, square, tanh, half = gelu_parts(pre)
        hb = bf(hidden)
        hid_ref[:, at] = hb
        residual_ref[:, at] = bf(centre[:, at] + dot(contract, hb))
        slope = half + (0.5 * GELU_A) * pre * (1.0 - tanh * tanh) * (1.0 + (3.0 * GELU_B) * square)
        slope_ref[:, at] = bf(slope)
        normed_ref[:, at] = normed
        inverse_ref[:, at] = jnp.broadcast_to(inverse, (8, REPLAY_CHUNK))


def block_backward(keep, turned, dy, grow):
    normed_ref, inverse_ref, _, slope_ref, _ = keep
    expand_t, contract_t, decoder_t = turned
    dpre_ref, dres_ref = grow
    dmixes, dress = [], []
    for c in range(0, dy.shape[1], BACKWARD_CHUNK):
        at = slice(c, c + BACKWARD_CHUNK)
        dres_b = bf(dot(decoder_t, bf(dy[:, at])))
        dhid = rounded(dot(contract_t, dres_b))
        dpre = bf(dhid * slope_ref[:, at].astype(F32))
        dn = rounded(dot(expand_t, dpre))
        normed = normed_ref[:, at]
        dmix = inverse_ref[0:1, at] * (
            dn
            - jnp.mean(dn, axis=0, keepdims=True)
            - normed * jnp.mean(dn * normed, axis=0, keepdims=True)
        )
        dpre_ref[:, at] = dpre
        dres_ref[:, at] = dres_b
        dmixes.append(dmix)
        dress.append(dres_b.astype(F32))
    join = lambda parts: jnp.concatenate(parts, axis=1)
    return join(dmixes), join(dress)


def feature_cotangent(dmix, dres, dw_ref, width, flags_ref, fold):
    rows = dres.shape[1] // width
    shifted = [rolled(dmix, width, by) for by in (1, 0, -1)]
    parts = []
    for i in range(3):
        terms = [shifted[j] * dw_ref[:, 3 * i + j : 3 * i + j + 1] for j in range(3)]
        parts.append(terms[0] + terms[1] + terms[2])
    empty = jnp.zeros((dmix.shape[0], width), F32)
    total = jnp.concatenate([parts[0], empty, empty], axis=1)
    total = total + jnp.concatenate([empty, parts[1] + dres, empty], axis=1)
    total = total + jnp.concatenate([empty, empty, parts[2]], axis=1)
    below = jnp.where(flags_ref[0] > 0, 0.0, total[:, :width])
    inner = total[:, width : (rows + 1) * width]
    over = total[:, (rows + 1) * width :]
    if fold is not None:
        back = dot_nt(bf(over), fold)
        top = inner[:, (rows - 1) * width :]
        top = jnp.where(flags_ref[1] > 0, top + back, top)
        inner = jnp.concatenate([inner[:, : (rows - 1) * width], top], axis=1)
    above = jnp.where(flags_ref[1] > 0, 0.0, over)
    return jnp.concatenate([below, inner, above], axis=1)


def input_cotangent(dfeat, enc_t_ref, width, flags_ref, fold):
    rows = dfeat.shape[1] // width - 2
    span = rows * width
    lowered = bf(dfeat)
    spread = None
    for i in range(3):
        start = (2 - i) * width
        term = dot(enc_t_ref[i], lowered[:, start : start + span])
        spread = term if spread is None else spread + term

    def gathered(spread):
        kinds = spread.shape[0] // 3
        parts = [rolled(spread[j * kinds : (j + 1) * kinds], width, 1 - j) for j in range(3)]
        return parts[0] + parts[1] + parts[2]

    dx = gathered(spread)
    if fold is not None:
        over = gathered(dot(enc_t_ref[2], lowered[:, rows * width : (rows + 1) * width]))
        back = dot_nt(bf(over), fold)
        top = dx[:, (rows - 1) * width :]
        top = jnp.where(flags_ref[1] > 0, top + back, top)
        dx = jnp.concatenate([dx[:, : (rows - 1) * width], top], axis=1)
    return dx


def depthwise_terms(dmix, shifted, width):
    span = dmix.shape[1]
    return [
        jnp.sum(dmix * shifted[j][:, i * width : i * width + span], axis=1, keepdims=True)
        for i in range(3)
        for j in range(3)
    ]


def send_edges(dfa, dfs, wa, ws, near, far, odd):
    up = jnp.concatenate([dfa[:, -2 * wa :], dfs[:, -2 * ws :]], axis=1)
    dn = jnp.concatenate([dfa[:, : 2 * wa], dfs[:, : 2 * ws]], axis=1)
    beside, other = sides(up, dn, odd)
    near[...] = bf(beside)
    far[...] = bf(other)


def backward_of(flags_ref, keeps, turned, dys, grows, dws, widths, fold, outs):
    found = []
    for keep, turn, dy, grow, dw, width, matrix, (dy_out, dmix_out, dfeat_out) in zip(
        keeps, turned, dys, grows, dws, widths, (None, fold), outs[0:2]
    ):
        dy_out[...] = bf(dy)
        dmix, dres = block_backward(keep, turn, dy, grow)
        dmix_out[...] = dmix
        dfeat = feature_cotangent(dmix, dres, dw, width, flags_ref, matrix)
        dfeat_out[...] = dfeat
        found.append(dfeat)
    send_edges(*found, *widths, *outs[2], flags_ref[2] > 0)


def weight_terms(air, sea, widths):
    grads = []
    for model in (air, sea):
        normed, hid, residual, dpre, dres = model[0:5]
        grads.append(dot_nt(bf(normed[...]), dpre[...]))
        grads.append(dot_nt(dres[...], hid[...]))
    wa, ws = widths
    dfeat_a, dfeat_s = bf(air[7][...]), bf(sea[7][...])
    air_stack, sea_stack = air[8], sea[8]
    span = dfeat_s.shape[1]
    blank = jnp.zeros((64, 64), F32)
    for i in range(3):
        part = dot_nt(dfeat_s, sea_stack[:, i * ws : i * ws + span])
        grads.append(jnp.concatenate([part, blank], axis=1))
    span = dfeat_a.shape[1]
    nine = jnp.concatenate([air_stack[:, i * wa : i * wa + span] for i in range(3)], axis=0)
    rest = dot_nt(dfeat_a, jnp.concatenate([nine, jnp.zeros((112, span), BF)], axis=0))
    dy_a, dy_s = air[5][...], sea[5][...]
    cells = dy_a.shape[1]
    zero = lambda rows: jnp.zeros((rows, cells), BF)
    rest = rest + dot_nt(air[2][...], jnp.concatenate([zero(144), dy_a, zero(96)], axis=0))
    rest = rest + dot_nt(sea[2][...], jnp.concatenate([zero(160), dy_s, zero(48)], axis=0))
    columns = []
    for model, width in ((air, wa), (sea, ws)):
        feat = model[9][...].astype(F32)
        columns += depthwise_terms(model[6][...], [rolled(feat, width, by) for by in (-1, 0, 1)], width)
    lanes = iota((64, 256), 1)
    for t, column in enumerate(columns):
        rest = rest + jnp.where(lanes == 208 + t, column, 0.0)
    grads.append(rest)
    return grads


def fetch(pairs, sems):
    copies = [pltpu.make_async_copy(src, dst, sems.at[i]) for i, (src, dst) in enumerate(pairs)]
    for copy in copies:
        copy.start()
    for copy in copies:
        copy.wait()


def pack_kernel(flags_ref, *refs):
    sources, outs, held, sems = refs[:8], refs[8:13], refs[13:21], refs[21]
    fetch(list(zip(sources, held)), sems)
    counts_ref, air_ref, sea_ref, flux_ref, ac_ref, sc_ref, ssh_ref, ash_ref = held
    mine, near, far, at_a, at_b = outs
    a = load_rows(air_ref)
    o = load_rows(sea_ref)
    flux = load_rows(flux_ref)
    place = iota((8, LANE), 0) * LANE + iota((8, LANE), 1)
    used = jnp.concatenate([jnp.where(place < counts_ref[0:1, k : k + 1], 1.0, 0.0) for k in range(5)], axis=0)
    ac, sc = ac_ref[...], sc_ref[...]
    wair, wsea = ash_ref[...] * used, ssh_ref[...] * used
    wair_hi, wsea_hi = rounded(wair), rounded(wsea)
    kinds = [
        (ac >> 7).astype(F32), (ac & 127).astype(F32), (sc >> 7).astype(F32), (sc & 127).astype(F32),
        wair_hi, wair - wair_hi, wsea_hi, wsea - wsea_hi,
    ]
    line = lambda x, k: jnp.concatenate([x[8 * k + h : 8 * k + h + 1] for h in range(8)], axis=1)
    air_hi, air_lo, sea_hi, sea_lo, wah, wal, wsh, wsl = [[line(x, k) for k in range(5)] for x in kinds]
    raw = jnp.concatenate([flux, jnp.zeros_like(flux)], axis=0)
    raw = jnp.where(iota((8, 1), 0) == SURFACE, o[0:1], raw)
    heads = []
    for d, off in enumerate(OFFS):
        k, m = 2 + off, 2 - off
        local = [air_hi[k], air_lo[k], sea_hi[m], sea_lo[m], wsh[m], wsl[m], wah[m], wal[m]]
        mine[8 * d : 8 * d + 8] = jnp.concatenate(local, axis=0)
        stat = [sea_hi[k], sea_lo[k], air_hi[m], air_lo[m], wah[k], wal[k], wsh[k], wsl[k]]
        heads.append(jnp.concatenate([raw] + stat, axis=0))
    mine[40:56] = heads[2]
    first, second = sides(heads[4], heads[0], flags_ref[3] > 0)
    at_a[...] = bf(first)
    at_b[...] = bf(second)
    edge = 2 * air_ref.shape[2]
    up = jnp.concatenate([heads[3], band_rows(o, a[:, -edge:])], axis=0)
    dn = jnp.concatenate([heads[1], band_rows(o, a[:, :edge])], axis=0)
    beside, other = sides(up, dn, flags_ref[2] > 0)
    near[...] = bf(beside)
    far[...] = bf(other)


def band_rows(o, a_edge):
    blank = jnp.zeros((8, o.shape[1] - a_edge.shape[1]), F32)
    tail = jnp.concatenate([a_edge, blank], axis=1)
    return jnp.concatenate([o, tail, jnp.zeros_like(tail)], axis=0)


FORMS = {}
for _name, _parts, _rows, _columns in (
    ("aef", 3, 64, 48), ("sef", 3, 64, 192), ("aeb", 3, 48, 64), ("seb", 3, 192, 64),
    ("aex", 1, 256, 64), ("sex", 1, 256, 64), ("aco_t", 1, 256, 64), ("sco_t", 1, 256, 64),
    ("aco", 1, 64, 256), ("sco", 1, 64, 256), ("aex_t", 1, 64, 256), ("sex_t", 1, 64, 256),
    ("ade", 1, 16, 64), ("sde", 1, 48, 64), ("ade_t", 1, 64, 16), ("sde_t", 1, 64, 48),
    ("adw", 1, 64, 9), ("sdw", 1, 64, 9),
):
    _start = max([start + parts * rows for start, parts, rows, _ in FORMS.values()], default=0)
    FORMS[_name] = (_start, _parts, _rows, _columns)
FORM_ROWS = max(start + parts * rows for start, parts, rows, _ in FORMS.values())


def forms(ref, *names):
    found = []
    for name in names:
        start, parts, rows, columns = FORMS[name]
        pieces = [ref[start + rows * i : start + rows * (i + 1), 0:columns] for i in range(parts)]
        if name in ("adw", "sdw"):
            pieces = [piece.astype(F32) for piece in pieces]
        found.append(pieces if parts > 1 else pieces[0])
    return found


def prepare_kernel(*refs):
    sources, out, held, sems = refs[:8], refs[8], refs[9:17], refs[17]
    fetch(list(zip(sources, held)), sems)
    aenc, senc, aex_t, sex_t, aco, sco, sde, small = [ref[...] for ref in held]

    def put(name, value, part=0):
        start, _, rows, columns = FORMS[name]
        out[start + rows * part : start + rows * (part + 1), 0:columns] = bf(value)

    kinds = aenc.shape[1] // 9
    for name, weights, padded in (("a", aenc, 16), ("s", senc, 64)):
        column = iota((1, 3 * padded), 1)
        kind = column % padded
        if name == "a":
            last = kind == kinds - 1 + SURFACE
            kind = jnp.where(kind < kinds - 1, kind, jnp.where(last, kinds - 1, -(1 << 20)))
        else:
            kind = jnp.where(kind < senc.shape[1] // 9, kind, -(1 << 20))
        for i in range(3):
            wanted = (3 * i + column // padded) * (weights.shape[1] // 9) + kind
            picked = dot(weights, bf(jnp.where(iota((weights.shape[1], 1), 0) == wanted, 1.0, 0.0)))
            put(name + "ef", picked, i)
            put(name + "eb", picked.T, i)
    turn = lambda x: x.astype(F32).T
    for name, value in (("aex_t", aex_t), ("sex_t", sex_t), ("aco", aco), ("sco", sco), ("sde", sde)):
        put(name, value)
    for name, value in (("aex", aex_t), ("sex", sex_t), ("aco_t", aco), ("sco_t", sco), ("sde_t", sde)):
        put(name, turn(value))
    small = small.astype(F32)
    put("ade", small[0:16])
    put("ade_t", small[0:16].T)
    put("adw", small[16:32].T[:, 0:9])
    put("sdw", small[32:48].T[:, 0:9])


def couple_kernel(flags_ref, mine, near, far, at_a, at_b, _, lists_out, cpl_out):
    up, dn = sides(near[0:16, :].astype(F32), far[0:16, :].astype(F32), flags_ref[2] > 0)
    up2, dn2 = sides(at_a[...].astype(F32), at_b[...].astype(F32), flags_ref[3] > 0)
    heads = [up2, up, mine[40:56], dn, dn2]
    lists = []
    for d, head in enumerate(heads):
        local = mine[8 * d : 8 * d + 8]
        stat = head[8:16]
        lists.append(
            jnp.concatenate([stat[0:2], local[0:2], stat[2:4], local[2:4], stat[4:8], local[4:8]], axis=0)
        )
    lists_out[...] = bf(jnp.concatenate(lists, axis=0))
    cpl = couple([full_paths(rows, True) for rows in lists], [to_table(head[0:CHANNELS]) for head in heads])
    cpl_out[...] = bf(jnp.concatenate([cpl, jnp.zeros_like(cpl)], axis=0))


def couple_again_kernel(place, lists_ref, own, near, at_a, at_b, a_ref, o_ref, cpl_out, near_out, far_out):
    cpl = couple(own_paths(lists_ref, True), tables_around(place, own, near, at_a, at_b))
    cpl_out[...] = bf(jnp.concatenate([cpl, jnp.zeros_like(cpl)], axis=0))
    a, o = a_ref[...], o_ref[...]
    edge = 2 * LANE
    blank = jnp.zeros((8, o.shape[1] - edge), F32)
    for out, rows in zip((near_out, far_out), sides(a[:, -edge:], a[:, :edge], place[2] > 0)):
        out[0:16, :] = bf(jnp.concatenate([cpl, jnp.concatenate([rows, blank], axis=1)], axis=0))
        out[16:64, :] = bf(o)


def model_inputs(a, o, cpl, bands, cpls):
    edge = 2 * LANE
    rows = iota((8, 1), 0)

    def joined(state_a, state_o, coupled, part):
        air = jnp.where(rows == SURFACE, coupled, 0.0)
        air = air if part is None else air[:, part]
        sea = jnp.where(rows < SURFACE, coupled, 0.0)
        return (
            jnp.concatenate([state_a, air], axis=0),
            jnp.concatenate([state_o, sea, jnp.zeros_like(sea)], axis=0),
        )

    below = joined(bands[0][48:56, :edge], bands[0][0:48], cpls[0], slice(-edge, None))
    above = joined(bands[1][48:56, :edge], bands[1][0:48], cpls[1], slice(0, edge))
    own = joined(a, o, cpl, None)
    return (
        jnp.concatenate([below[0], own[0], above[0]], axis=1),
        jnp.concatenate([below[1], own[1], above[1]], axis=1),
    )


def wet_rows(wet_ref):
    wet = wet_ref[...].astype(F32)
    return jnp.concatenate([wet[r : r + 1] for r in range(wet.shape[0])], axis=1)


def put_table(out, raw):
    out[...] = bf(jnp.concatenate([to_table(raw), jnp.zeros((8, LANE), F32)], axis=0))


def forward_kernel(
    flags_ref, air_ref, o_ref, cpl_ref, band_near, band_far, cpl_near, cpl_far, wet_ref, partner_ref,
    weights_ref, a_out, o_out, table_out, air_stack_out, sea_stack_out, air_feat_out, sea_feat_out,
):
    aef, sef, adw, aex, aco, ade, sdw, sex, sco, sde = forms(
        weights_ref, "aef", "sef", "adw", "aex", "aco", "ade", "sdw", "sex", "sco", "sde"
    )
    wa, ws = LANE, wet_ref.shape[1]
    odd = flags_ref[2] > 0
    a, o = load_rows(air_ref), load_rows(o_ref)
    fold = fold_matrix(partner_ref)
    above, below = sides(band_near[...].astype(F32)[16:80], band_far[...].astype(F32)[16:80], odd)
    cpl_up, cpl_dn = sides(cpl_near[...].astype(F32)[0:8], cpl_far[...].astype(F32)[0:8], odd)
    cpl = cpl_ref[...].astype(F32)[0:8]
    xa, xs = model_inputs(a, o, cpl, (below, above), (cpl_dn, cpl_up))
    air_stack, air_feat = features_of(xa, aef, wa, flags_ref, None)
    sea_stack, sea_feat = features_of(xs, sef, ws, flags_ref, fold)
    air_stack_out[...] = air_stack
    sea_stack_out[...] = sea_stack
    air_feat_out[...] = bf(air_feat)
    sea_feat_out[...] = bf(sea_feat)
    y_air = block_forward(mix(air_feat, adw, wa)[0], air_feat[:, wa:-wa], aex[...], aco[...], ade[...])
    y_sea = block_forward(mix(sea_feat, sdw, ws)[0], sea_feat[:, ws:-ws], sex[...], sco[...], sde[...])
    a = a + y_air[0:8]
    o = o + wet_rows(wet_ref) * y_sea
    a_out[...] = a
    o_out[...] = o
    put_table(table_out, jnp.concatenate([y_air[8:12], o[0:1]], axis=0))


def last_kernel(
    flags_ref, a_ref, o_ref, cpl_ref, band_near, band_far, wet_ref, partner_ref,
    acot_ref, ocot_ref, weights_ref,
    a_out, o_out, air_stack_out, sea_stack_out, air_feat_out, sea_feat_out,
    na, ia, ha, la, ra, ns, is_, hs, ls, rs, pa, ea, ps, es,
    dya, dma, dfa, dys, dms, dfs, near, far,
):
    aef, sef, adw, aex, aco, ade, sdw, sex, sco, sde = forms(
        weights_ref, "aef", "sef", "adw", "aex", "aco", "ade", "sdw", "sex", "sco", "sde"
    )
    aex_t, aco_t, ade_t, sex_t, sco_t, sde_t = forms(weights_ref, "aex_t", "aco_t", "ade_t", "sex_t", "sco_t", "sde_t")
    wa, ws = LANE, wet_ref.shape[1]
    odd = flags_ref[2] > 0
    a, o = a_ref[...], o_ref[...]
    fold = fold_matrix(partner_ref)
    up, dn = sides(band_near[...].astype(F32), band_far[...].astype(F32), odd)
    below, above = [jnp.concatenate([band[16:64], band[8:16]], axis=0) for band in (dn, up)]
    cpl = cpl_ref[...].astype(F32)[0:8]
    xa, xs = model_inputs(a, o, cpl, (below, above), (dn[0:8], up[0:8]))
    air_stack, air_feat = features_of(xa, aef, wa, flags_ref, None)
    sea_stack, sea_feat = features_of(xs, sef, ws, flags_ref, fold)
    air_stack_out[...] = air_stack
    sea_stack_out[...] = sea_stack
    air_feat_out[...] = bf(air_feat)
    sea_feat_out[...] = bf(sea_feat)
    keeps = ((na, ia, ha, la, ra), (ns, is_, hs, ls, rs))
    block_replay(mix(air_feat, adw, wa)[0], air_feat[:, wa:-wa], aex[...], aco[...], keeps[0])
    block_replay(mix(sea_feat, sdw, ws)[0], sea_feat[:, ws:-ws], sex[...], sco[...], keeps[1])
    wet = wet_rows(wet_ref)
    acot = load_rows(acot_ref)
    turned = ((aex_t[...], aco_t[...], ade_t[...]), (sex_t[...], sco_t[...], sde_t[...]))
    backward_of(
        flags_ref, keeps, turned, (jnp.concatenate([acot, jnp.zeros_like(acot)], axis=0), wet * load_rows(ocot_ref)),
        ((pa, ea), (ps, es)), (adw, sdw), (wa, ws), fold, ((dya, dma, dfa), (dys, dms, dfs), (near, far)),
    )
    store_rows(a_out, a + dot(ade[...], ra[...])[0:8])
    store_rows(o_out, o + wet * dot(sde[...], rs[...]))


def replay_kernel(
    air_feat_ref, sea_feat_ref, weights_ref, na, ia, ha, la, ra, ns, is_, hs, ls, rs,
):
    adw, aex, aco, sdw, sex, sco = forms(weights_ref, "adw", "aex", "aco", "sdw", "sex", "sco")
    for feat_ref, dw, ex, co, keep in (
        (air_feat_ref, adw, aex, aco, (na, ia, ha, la, ra)),
        (sea_feat_ref, sdw, sex, sco, (ns, is_, hs, ls, rs)),
    ):
        feat = feat_ref[...].astype(F32)
        width = (feat.shape[1] - na.shape[1]) // 2
        block_replay(mix(feat, dw, width)[0], feat[:, width:-width], ex[...], co[...], keep)


def first_kernel(
    flags_ref, lists_ref, own, t_near, at_a, at_b, acot_ref, ocot_ref, wet_ref, partner_ref,
    na, ia, ha, la, ra, ns, is_, hs, ls, rs, weights_ref,
    ocot_out, pa, ea, ps, es, dya, dma, dfa, dys, dms, dfs, near, far,
):
    adw, sdw = forms(weights_ref, "adw", "sdw")
    aex_t, aco_t, ade_t, sex_t, sco_t, sde_t = forms(weights_ref, "aex_t", "aco_t", "ade_t", "sex_t", "sco_t", "sde_t")
    wa, ws = LANE, wet_ref.shape[1]
    fold = fold_matrix(partner_ref)
    tables = tables_around(flags_ref, own, t_near, at_a, at_b)
    at_air, at_sea = regrid(own_paths(lists_ref, False), tables, False)
    ocot = ocot_ref[...]
    ocot = jnp.where(iota((ocot.shape[0], 1), 0) == 0, ocot + at_sea, ocot)
    ocot_out[...] = ocot
    flux_rows = jnp.concatenate([at_air, jnp.zeros_like(at_air)], axis=0)
    turned = ((aex_t[...], aco_t[...], ade_t[...]), (sex_t[...], sco_t[...], sde_t[...]))
    backward_of(
        flags_ref, ((na, ia, ha, la, ra), (ns, is_, hs, ls, rs)), turned,
        (jnp.concatenate([acot_ref[...], flux_rows], axis=0), wet_rows(wet_ref) * ocot),
        ((pa, ea), (ps, es)), (adw, sdw), (wa, ws), fold, ((dya, dma, dfa), (dys, dms, dfs), (near, far)),
    )


def last_grads_kernel(*refs):
    air, sea, out, done = refs[0:10], refs[10:20], refs[20], refs[21]
    done[...] = jnp.zeros_like(done)
    widths = LANE, (sea[9].shape[1] - sea[0].shape[1]) // 2
    out[...] = jnp.concatenate(weight_terms(air, sea, widths), axis=1)


def first_grads_kernel(*refs):
    air, sea, later, out, done = refs[0:10], refs[10:20], refs[20], refs[22], refs[23]
    done[...] = jnp.zeros_like(done)
    widths = LANE, (sea[9].shape[1] - sea[0].shape[1]) // 2
    for p, grad in enumerate(weight_terms(air, sea, widths)):
        total = bf(later[:, 256 * p : 256 * p + 256] + grad)
        for q in range(4):
            for l in range(2):
                row = 16 * (16 * q + 2 * p + l)
                out[row : row + 16, :] = total[16 * q : 16 * q + 16, LANE * l : LANE * (l + 1)]


def input_kernel(
    flags_ref, dfa_ref, dfs_ref, from_near, from_far, acot_ref, ocot_ref, partner_ref, weights_ref, *refs,
):
    acot_out, ocot_out, table_out = refs[-3:]
    aeb, seb = forms(weights_ref, "aeb", "seb")
    wa, ws = LANE, partner_ref.shape[1]
    fold = fold_matrix(partner_ref)
    up, dn = sides(from_near[...].astype(F32), from_far[...].astype(F32), flags_ref[2] > 0)
    dfa, dfs = dfa_ref[...], dfs_ref[...]
    middle = jnp.zeros((64, dfa.shape[1] - 4 * wa), F32)
    dfa = dfa + jnp.concatenate([dn[:, : 2 * wa], middle, up[:, : 2 * wa]], axis=1)
    dfs = dfs + jnp.concatenate([dn[:, 2 * wa :], up[:, 2 * wa :]], axis=1)
    dxa = input_cotangent(dfa, aeb, wa, flags_ref, None)
    dxs = input_cotangent(dfs, seb, ws, flags_ref, fold)
    if len(acot_ref.shape) == 3:
        acot_out[...] = load_rows(acot_ref) + dxa[0:8]
        ocot_out[...] = load_rows(ocot_ref) + dxs[0:48]
    else:
        store_rows(acot_out, acot_ref[...] + dxa[0:8])
        ocot_out[...] = ocot_ref[...] + dxs[0:48]
    put_table(table_out, jnp.concatenate([dxs[48:52], dxa[12:13]], axis=0))


def total_kernel(terms_ref, _, out):
    total = terms_ref[0].astype(F32)
    for i in range(1, terms_ref.shape[0]):
        total = total + terms_ref[i].astype(F32)
    total = bf(total)
    for i in range(out.shape[0]):
        out[i] = total


def final_kernel(flags_ref, lists_ref, own, near, at_a, at_b, ocot_ref, sea_out, flux_out):
    tables = tables_around(flags_ref, own, near, at_a, at_b)
    at_air, at_sea = regrid(own_paths(lists_ref, False), tables, False)
    ocot = ocot_ref[...]
    ocot = jnp.where(iota((ocot.shape[0], 1), 0) == 0, ocot + at_sea, ocot)
    store_rows(sea_out, ocot)
    store_rows(flux_out, at_air)


def unpack_kernel(
    air_scale, sea_scale, sums_ref, acol_ref, scol_ref, ae, adw, aex, aco, ade, se, sdw, sex, sco, sde,
):
    sums = jnp.concatenate([sums_ref[i].astype(F32) for i in range(sums_ref.shape[0])], axis=0)

    def part(p):
        lanes = []
        for l in range(2):
            rows = [16 * (16 * q + 2 * p + l) for q in range(4)]
            lanes.append(jnp.concatenate([sums[row : row + 16] for row in rows], axis=0))
        return jnp.concatenate(lanes, axis=1)

    aex[...] = part(0) * air_scale
    aco[...] = part(1) * air_scale
    sex[...] = part(2) * sea_scale
    sco[...] = part(3) * sea_scale

    def picked(block, wanted, base):
        chosen = bf(jnp.where(iota((256, wanted.shape[1]), 0) + base == wanted, 1.0, 0.0))
        return dot(bf(block), chosen)

    columns = scol_ref[...]
    se[...] = sea_scale * (picked(part(4), columns, 0) + picked(part(5), columns, 256) + picked(part(6), columns, 512))
    rest = part(7)
    ae[...] = air_scale * picked(rest, acol_ref[...], 0)
    across = rest.T
    adw[...] = air_scale * across[208 : 208 + adw.shape[0]]
    sdw[...] = sea_scale * across[217 : 217 + sdw.shape[0]]
    ade[...] = air_scale * across[144 : 144 + ade.shape[0]]
    sde[...] = sea_scale * across[160 : 160 + sde.shape[0]]


VMEM = pl.BlockSpec(memory_space=pltpu.VMEM)


def place():
    position, count = lax.axis_index("tile"), lax.axis_size("tile")
    return [jnp.int32(0) + x for x in (position == 0, position == count - 1, position % 2, position // 2 % 2)]


def placed_kernel(kernel):
    return lambda *refs: kernel(place(), *refs)


def call(kernel, name, outs, args, scratch=(), specs=None, cost=None, limit=VMEM_LIMIT):
    return pl.pallas_call(
        kernel,
        out_shape=[jax.ShapeDtypeStruct(shape, kind) for shape, kind in outs],
        in_specs=specs or [VMEM] * len(args),
        out_specs=[VMEM] * len(outs),
        scratch_shapes=list(scratch),
        compiler_params=pltpu.CompilerParams(vmem_limit_bytes=limit),
        cost_estimate=cost and pl.CostEstimate(flops=int(cost), bytes_accessed=4 << 20, transcendentals=0),
        name=name,
    )(*args)


def chips_beside(at_a, at_b):
    length = lax.axis_size("tile")
    first = [(i, i ^ 2) for i in range(length)]
    second = [(i, j) for i in range(length) for j in [((i + 2) ^ 2) - 2] if 0 <= j < length]
    at_b = lax.ppermute(at_b, "tile", second)
    return lax.ppermute(at_a, "tile", first), at_b


def beside(near, far):
    length = lax.axis_size("tile")
    chip = [(i, i ^ 1) for i in range(length)]
    other = [(i, j) for i in range(length) for j in [((i + 1) ^ 1) - 1] if 0 <= j < length]
    far = lax.ppermute(far, "tile", other)
    return lax.ppermute(near, "tile", chip), far


def to_all(blocks):
    return lax.all_to_all(blocks, "tile", 0, 0)


def around(table):
    length = lax.axis_size("tile")
    near = lax.ppermute(table, "tile", [(i, i ^ 1) for i in range(length)])
    pair = jnp.concatenate([table, near], axis=0)
    return (table, near, *chips_beside(pair, pair))


def body(
    air_state, sea_state, flux_start, air_cells, sea_cells, slot_counts, sea_share, air_share,
    polar_fold_partner, wet_mask, air_cotangent, sea_cotangent,
    air_encoder, air_depthwise, air_expand, air_contract, air_decoder,
    sea_encoder, sea_depthwise, sea_expand, sea_contract, sea_decoder,
):
    devices = lax.axis_size("tile")
    ach, air_rows, air_width = air_state.shape
    och, sea_rows, sea_width = sea_state.shape
    flux = flux_start.shape[0]
    slots = air_cells.shape[2]
    air_sites, sea_sites = air_rows * air_width, sea_rows * sea_width
    partner = polar_fold_partner.reshape(1, sea_width)

    air_columns, sea_columns = [], []
    for t in range(9):
        i, j = divmod(t, 3)
        air_columns += [48 * i + 16 * j + (k if k < ach else ach + SURFACE) for k in range(ach + 1)]
        sea_columns += [256 * i + 64 * j + k for k in range(och + flux)]
    air_columns, sea_columns = np.array([air_columns], np.int32), np.array([sea_columns], np.int32)

    lines = lambda x: x.reshape(-1, LANE)
    sources = (
        slot_counts, air_state, sea_state, flux_start,
        lines(air_cells), lines(sea_cells), lines(sea_share), lines(air_share),
    )
    head = ((16, sea_sites), BF)
    band = ((80, sea_sites), BF)
    mine, near, far, at_a, at_b = call(
        placed_kernel(pack_kernel), "pack",
        [((56, slots), F32), band, band, head, head],
        sources,
        specs=[pl.BlockSpec(memory_space=pltpu.HBM)] * len(sources),
        limit=60 * 1024 * 1024,
        scratch=[pltpu.VMEM(x.shape, x.dtype) for x in sources] + [pltpu.SemaphoreType.DMA((len(sources),))],
    )
    band_near, band_far = beside(near, far)
    at_a, at_b = chips_beside(at_a, at_b)
    rows_of = lambda x, count: jnp.pad(x, ((0, count - x.shape[0]), (0, 0)))
    small = [rows_of(air_decoder, 16), rows_of(air_depthwise.T, 16), rows_of(sea_depthwise.T, 16)]
    sources = (
        air_encoder, sea_encoder, air_expand.T, sea_expand.T, air_contract, sea_contract, sea_decoder,
        jnp.concatenate(small, axis=0),
    )
    (weights,) = call(
        prepare_kernel, "prepare", [((FORM_ROWS, 256), BF)], sources,
        specs=[pl.BlockSpec(memory_space=pltpu.HBM)] * len(sources), limit=60 * 1024 * 1024, cost=3e9,
        scratch=[pltpu.VMEM(x.shape, x.dtype) for x in sources] + [pltpu.SemaphoreType.DMA((len(sources),))],
    )
    lists, cpl = call(
        placed_kernel(couple_kernel), "couple", [((80, slots), BF), head],
        (mine, band_near, band_far, at_a, at_b, weights),
        specs=[VMEM] * 5 + [pl.BlockSpec(memory_space=pltpu.HBM)],
    )
    cpl_near, cpl_far = beside(cpl, cpl)
    stacks = [((48, (air_rows + 4) * air_width), BF), ((192, (sea_rows + 4) * sea_width), BF)]
    feats = [((64, (air_rows + 2) * air_width), BF), ((64, (sea_rows + 2) * sea_width), BF)]
    keeps, grows, backs = [], [], []
    for sites, outputs, (feat, _) in ((air_sites, 16, feats[0]), (sea_sites, och, feats[1])):
        keeps += [((64, sites), F32), ((8, sites), F32), ((256, sites), BF), ((256, sites), BF), ((64, sites), BF)]
        grows += [((256, sites), BF), ((64, sites), BF)]
        backs += [((outputs, sites), BF), ((64, sites), F32), (feat, F32)]
    halo = ((64, 2 * air_width + 2 * sea_width), BF)
    table = ((48, LANE), BF)
    state = ((64, sea_sites), BF)
    a1, o1, own, ast, sst, aft, sft = call(
        placed_kernel(forward_kernel), "forward",
        [((ach, air_sites), F32), ((och, sea_sites), F32), table, *stacks, *feats],
        (air_state, sea_state, cpl, band_near, band_far, cpl_near, cpl_far, wet_mask, partner, weights),
    )
    cpl, near, far = call(
        placed_kernel(couple_again_kernel), "couple_again", [head, state, state], (lists, *around(own), a1, o1)
    )
    band_near, band_far = beside(near, far)
    air_final, sea_final, ast1, sst1, aft1, sft1, *rest = call(
        placed_kernel(last_kernel), "last",
        [(air_state.shape, F32), (sea_state.shape, F32), *stacks, *feats, *keeps, *grows, *backs, halo, halo],
        (a1, o1, cpl, band_near, band_far, wet_mask, partner, air_cotangent, sea_cotangent,
         weights),
    )
    keep, (pa, ea, ps, es, dya, dma, dfa, dys, dms, dfs, near, far) = rest[:10], rest[10:]
    edge_near, edge_far = beside(near, far)
    gathered = lambda keep, pa, ea, ps, es, dya, dma, dfa, dys, dms, dfs, ast, sst, aft, sft: (
        keep[0], keep[2], keep[4], pa, ea, dya, dma, dfa, ast, aft,
        keep[5], keep[7], keep[9], ps, es, dys, dms, dfs, sst, sft,
    )
    token = ((8, LANE), F32)
    later, done = call(
        last_grads_kernel, "last_grads", [((64, 2048), F32), token],
        gathered(keep, pa, ea, ps, es, dya, dma, dfa, dys, dms, dfs, ast1, sst1, aft1, sft1), cost=3e9,
    )
    acot, ocot, own = call(
        placed_kernel(input_kernel), "inputs", [((ach, air_sites), F32), ((och, sea_sites), F32), table],
        (dfa, dfs, edge_near, edge_far, air_cotangent, sea_cotangent, partner, weights, done),
    )

    keep = call(
        replay_kernel, "replay", keeps, (aft, sft, weights), cost=3e9
    )
    ocot, pa, ea, ps, es, dya, dma, dfa, dys, dms, dfs, near, far = call(
        placed_kernel(first_kernel), "first", [((och, sea_sites), F32), *grows, *backs, halo, halo],
        (lists, *around(own), acot, ocot, wet_mask, partner, *keep, weights),
    )
    edge_near, edge_far = beside(near, far)
    grads, done = call(
        first_grads_kernel, "first_grads", [((8 * LANE, LANE), BF), token],
        (*gathered(keep, pa, ea, ps, es, dya, dma, dfa, dys, dms, dfs, ast, sst, aft, sft), later, edge_near), cost=3e9,
    )
    terms = to_all(grads.reshape(devices, -1, LANE))
    air_grad, ocot, own = call(
        placed_kernel(input_kernel), "first_inputs", [(air_state.shape, F32), ((och, sea_sites), F32), table],
        (dfa, dfs, edge_near, edge_far, acot, ocot, partner, weights, done), cost=5e10,
    )
    tables = around(own)
    (sums,) = call(total_kernel, "total", [(terms.shape, BF)], (terms, tables[2]))
    sums = to_all(sums)
    sea_grad, flux_grad = call(
        placed_kernel(final_kernel), "final", [(sea_state.shape, F32), (flux_start.shape, F32)],
        (lists, *tables, ocot), cost=5e10,
    )
    air_scale = 1.0 / math.sqrt(air_sites * devices)
    sea_scale = 1.0 / math.sqrt(sea_sites * devices)
    flipped = lambda w: (w.shape[1], w.shape[0])
    shapes = [
        air_encoder.shape, flipped(air_depthwise), flipped(air_expand), air_contract.shape, air_decoder.shape,
        sea_encoder.shape, flipped(sea_depthwise), flipped(sea_expand), sea_contract.shape, sea_decoder.shape,
    ]
    ae, dwa, exa, coa, dea, se, dws, exs, cos, des = call(
        lambda *refs: unpack_kernel(air_scale, sea_scale, *refs), "unpack", [(shape, F32) for shape in shapes],
        (sums, air_columns, sea_columns),
    )
    return (
        air_final, sea_final, air_grad, sea_grad, flux_grad,
        ae, dwa.T, exa.T, coa, dea, se, dws.T, exs.T, cos, des,
    )


def solution(mesh):
    rows = P(None, "tile", None)
    blocks = P("tile", None, None)
    placed = (
        (rows,) * 3 + (blocks,) * 2 + (P("tile", None),) + (blocks,) * 2 + (P(), P("tile", None)) + (rows,) * 2 + (P(),) * 10
    )
    return jax.shard_map(
        body, mesh=mesh, in_specs=placed, out_specs=(rows,) * 5 + (P(),) * 10, check_vma=False
    )
```

```python
import math

import jax
import jax.numpy as jnp
import numpy as np
from jax import lax
from jax.experimental import pallas as pl
from jax.experimental.pallas import tpu as pltpu
from jax.sharding import PartitionSpec as P

F32 = jnp.float32
BF = jnp.bfloat16
OFFS = (-2, -1, 0, 1, 2)
LANE = 128
FORWARD_CHUNK, REPLAY_CHUNK, BACKWARD_CHUNK = 1024, 1024, 1024
VMEM_LIMIT = 16 * 1024 * 1024
SURFACE = 4
CHANNELS = 5


def dot(a, b):
    return lax.dot_general(a, b, (((1,), (0,)), ((), ())), preferred_element_type=F32)


def dot_nt(a, b):
    return lax.dot_general(a, b, (((1,), (1,)), ((), ())), preferred_element_type=F32)


def dot_tn(a, b):
    return lax.dot_general(a, b, (((0,), (0,)), ((), ())), preferred_element_type=F32)


def bf(x):
    return x.astype(BF)


def rounded(x):
    return x.astype(BF).astype(F32)


def iota(shape, axis):
    return lax.broadcasted_iota(jnp.int32, shape, axis)


def load_rows(ref):
    return jnp.concatenate([ref[:, r, :] for r in range(ref.shape[1])], axis=1)


def store_rows(ref, x):
    width = ref.shape[2]
    for r in range(ref.shape[1]):
        ref[:, r, :] = x[:, r * width : (r + 1) * width]


def rolled(x, width, by):
    if by == 0:
        return x
    rows = x.shape[1] // width
    return jnp.concatenate(
        [pltpu.roll(x[:, r * width : (r + 1) * width], (-by) % width, 1) for r in range(rows)], axis=1
    )


def onehot(low):
    return jnp.where(bf(iota((LANE, 1), 0)) == bf(low), jnp.ones((), BF), jnp.zeros((), BF))


def to_table(raw):
    pieces = []
    for ch in range(CHANNELS):
        pieces += [raw[ch : ch + 1, LANE * h : LANE * (h + 1)] for h in range(8)]
    return jnp.concatenate(pieces, axis=0)


def from_table(table):
    rows = []
    for ch in range(table.shape[0] // 8):
        rows.append(jnp.concatenate([table[8 * ch + h : 8 * ch + h + 1] for h in range(8)], axis=1))
    return jnp.concatenate(rows, axis=0) if len(rows) > 1 else rows[0]


def moved(table, path):
    from_hi, from_lo, to_hi, to_lo, weight = path
    gathered = dot(bf(table), onehot(from_lo))
    rows = iota((8, 1), 0).astype(F32)
    picks, puts = rows == from_hi, rows == to_hi
    spread = []
    for g in range(0, table.shape[0], 8):
        value = jnp.sum(jnp.where(picks, gathered[g : g + 8], 0.0), axis=0, keepdims=True) * weight
        spread.append(jnp.where(puts, value, 0.0))
    return dot_nt(bf(jnp.concatenate(spread, axis=0)), onehot(to_lo))


def full_paths(rows, forward):
    line = lambda i: rows[i : i + 1]
    base = 8 if forward else 10
    air = [line(i) for i in range(4)] + [line(base) + line(base + 1)]
    sea = [line(i) for i in range(4, 8)] + [line(base + 4) + line(base + 5)]
    return air, sea


def regrid(paths, tables, forward):
    at_air = at_sea = None
    for (to_air, to_sea), table in zip(paths, tables):
        surface, fluxes = table[8 * SURFACE :], table[: 8 * SURFACE]
        first, second = (surface, fluxes) if forward else (fluxes, surface)
        air = moved(first, to_air)
        sea = moved(second, to_sea)
        at_air = air if at_air is None else at_air + air
        at_sea = sea if at_sea is None else at_sea + sea
    return from_table(at_air), from_table(at_sea)


def own_paths(lists_ref, forward):
    lists = lists_ref[...].astype(F32)
    return [full_paths(lists[16 * d : 16 * d + 16], forward) for d in range(len(OFFS))]


def tables_around(flags_ref, own, near, at_a, at_b):
    own, near, at_a, at_b = [ref[...].astype(F32) for ref in (own, near, at_a, at_b)]
    odd, odd_chip = flags_ref[2] > 0, flags_ref[3] > 0
    up, dn = jnp.where(odd_chip, at_b, at_a), jnp.where(odd_chip, at_a, at_b)
    above = jnp.where(odd, up[48:88], near[0:40])
    below = jnp.where(odd, near[0:40], dn[48:88])
    return [up[0:40], above, own[0:40], below, dn[0:40]]


def couple(paths, tables):
    at_air, at_sea = regrid(paths, tables, True)
    return jnp.concatenate([at_sea, at_air, jnp.zeros((3, at_air.shape[1]), F32)], axis=0)


def sides(near, far, odd):
    return jnp.where(odd, far, near), jnp.where(odd, near, far)


def fold_matrix(partner_ref):
    columns = partner_ref.shape[1]
    return bf(jnp.where(iota((columns, columns), 0) == partner_ref[...], 1.0, 0.0))


def features_of(x, enc_ref, width, flags_ref, fold):
    rows = x.shape[1] // width - 4
    if fold is not None:
        top = x[:, (rows + 1) * width : (rows + 2) * width]
        above = x[:, (rows + 2) * width : (rows + 3) * width]
        above = jnp.where(flags_ref[1] > 0, dot(bf(top), fold), above)
        x = jnp.concatenate([x[:, : (rows + 2) * width], above, x[:, (rows + 3) * width :]], axis=1)
    stack = jnp.concatenate([bf(rolled(x, width, by)) for by in (-1, 0, 1)], axis=0)
    span = (rows + 2) * width
    feat = dot(enc_ref[0], stack[:, 0:span])
    for i in (1, 2):
        feat = feat + dot(enc_ref[i], stack[:, i * width : i * width + span])
    feat = rounded(feat)
    below = jnp.where(flags_ref[0] > 0, 0.0, feat[:, :width])
    above = feat[:, (rows + 1) * width :]
    if fold is not None:
        over = dot(bf(feat[:, rows * width : (rows + 1) * width]), fold)
    else:
        over = 0.0
    above = jnp.where(flags_ref[1] > 0, over, above)
    return stack, jnp.concatenate([below, feat[:, width : (rows + 1) * width], above], axis=1)


def mix(feat, dw_ref, width):
    rows = feat.shape[1] // width - 2
    span = rows * width
    shifted = [rolled(feat, width, by) for by in (-1, 0, 1)]
    total = None
    for i in range(3):
        for j in range(3):
            term = shifted[j][:, i * width : i * width + span] * dw_ref[:, 3 * i + j : 3 * i + j + 1]
            total = term if total is None else total + term
    return total, shifted


def normalise(mixed):
    centred = mixed - jnp.mean(mixed, axis=0, keepdims=True)
    inverse = lax.rsqrt(jnp.mean(centred * centred, axis=0, keepdims=True) + 1e-06)
    return centred * inverse, inverse


GELU_A = math.sqrt(2.0 / math.pi)
GELU_B = 0.044715


def gelu_parts(v):
    square = v * v
    tanh = jnp.tanh(GELU_A * v * (1.0 + GELU_B * square))
    half = 0.5 * (1.0 + tanh)
    return v * half, square, tanh, half


def block_forward(mixed, centre, expand, contract, decoder):
    outs = []
    for c in range(0, mixed.shape[1], FORWARD_CHUNK):
        normed, _ = normalise(mixed[:, c : c + FORWARD_CHUNK])
        hidden = gelu_parts(dot(expand, bf(normed)))[0]
        residual = centre[:, c : c + FORWARD_CHUNK] + dot(contract, bf(hidden))
        outs.append(dot(decoder, bf(residual)))
    return jnp.concatenate(outs, axis=1)


def block_replay(mixed, centre, expand, contract, keep):
    normed_ref, inverse_ref, hid_ref, slope_ref, residual_ref = keep
    for c in range(0, mixed.shape[1], REPLAY_CHUNK):
        at = slice(c, c + REPLAY_CHUNK)
        normed, inverse = normalise(mixed[:, at])
        pre = dot(expand, bf(normed))
        hidden, square, tanh, half = gelu_parts(pre)
        hb = bf(hidden)
        hid_ref[:, at] = hb
        residual_ref[:, at] = bf(centre[:, at] + dot(contract, hb))
        slope = half + (0.5 * GELU_A) * pre * (1.0 - tanh * tanh) * (1.0 + (3.0 * GELU_B) * square)
        slope_ref[:, at] = bf(slope)
        normed_ref[:, at] = normed
        inverse_ref[:, at] = jnp.broadcast_to(inverse, (8, REPLAY_CHUNK))


def block_backward(keep, weights, dy, grow):
    normed_ref, inverse_ref, _, slope_ref, _ = keep
    expand, contract, decoder = weights
    dpre_ref, dres_ref = grow
    dmixes, dress = [], []
    for c in range(0, dy.shape[1], BACKWARD_CHUNK):
        at = slice(c, c + BACKWARD_CHUNK)
        dres_b = bf(dot_tn(decoder, bf(dy[:, at])))
        dhid = rounded(dot_tn(contract, dres_b))
        dpre = bf(dhid * slope_ref[:, at].astype(F32))
        dn = rounded(dot_tn(expand, dpre))
        normed = normed_ref[:, at]
        dmix = inverse_ref[0:1, at] * (
            dn
            - jnp.mean(dn, axis=0, keepdims=True)
            - normed * jnp.mean(dn * normed, axis=0, keepdims=True)
        )
        dpre_ref[:, at] = dpre
        dres_ref[:, at] = dres_b
        dmixes.append(dmix)
        dress.append(dres_b.astype(F32))
    join = lambda parts: jnp.concatenate(parts, axis=1)
    return join(dmixes), join(dress)


def feature_cotangent(dmix, dres, dw_ref, width, flags_ref, fold):
    rows = dres.shape[1] // width
    shifted = [rolled(dmix, width, by) for by in (1, 0, -1)]
    parts = []
    for i in range(3):
        terms = [shifted[j] * dw_ref[:, 3 * i + j : 3 * i + j + 1] for j in range(3)]
        parts.append(terms[0] + terms[1] + terms[2])
    empty = jnp.zeros((dmix.shape[0], width), F32)
    total = jnp.concatenate([parts[0], empty, empty], axis=1)
    total = total + jnp.concatenate([empty, parts[1] + dres, empty], axis=1)
    total = total + jnp.concatenate([empty, empty, parts[2]], axis=1)
    below = jnp.where(flags_ref[0] > 0, 0.0, total[:, :width])
    inner = total[:, width : (rows + 1) * width]
    over = total[:, (rows + 1) * width :]
    if fold is not None:
        back = dot_nt(bf(over), fold)
        top = inner[:, (rows - 1) * width :]
        top = jnp.where(flags_ref[1] > 0, top + back, top)
        inner = jnp.concatenate([inner[:, : (rows - 1) * width], top], axis=1)
    above = jnp.where(flags_ref[1] > 0, 0.0, over)
    return jnp.concatenate([below, inner, above], axis=1)


def input_cotangent(dfeat, enc_ref, width, flags_ref, fold):
    rows = dfeat.shape[1] // width - 2
    span = rows * width
    lowered = bf(dfeat)
    spread = None
    for i in range(3):
        start = (2 - i) * width
        term = dot_tn(enc_ref[i], lowered[:, start : start + span])
        spread = term if spread is None else spread + term

    def gathered(spread):
        kinds = spread.shape[0] // 3
        parts = [rolled(spread[j * kinds : (j + 1) * kinds], width, 1 - j) for j in range(3)]
        return parts[0] + parts[1] + parts[2]

    dx = gathered(spread)
    if fold is not None:
        over = gathered(dot_tn(enc_ref[2], lowered[:, rows * width : (rows + 1) * width]))
        back = dot_nt(bf(over), fold)
        top = dx[:, (rows - 1) * width :]
        top = jnp.where(flags_ref[1] > 0, top + back, top)
        dx = jnp.concatenate([dx[:, : (rows - 1) * width], top], axis=1)
    return dx


def depthwise_terms(shifted, feat, width):
    span = shifted[0].shape[1]
    return [
        jnp.sum(shifted[j] * feat[:, i * width : i * width + span], axis=1, keepdims=True)
        for i in range(3)
        for j in range(3)
    ]


def send_edges(dfa, dfs, wa, ws, near, far, odd):
    up = jnp.concatenate([dfa[:, -2 * wa :], dfs[:, -2 * ws :]], axis=1)
    dn = jnp.concatenate([dfa[:, : 2 * wa], dfs[:, : 2 * ws]], axis=1)
    beside, other = sides(up, dn, odd)
    near[...] = bf(beside)
    far[...] = bf(other)


def backward_of(flags_ref, keeps, pointwise, dys, grows, dws, widths, fold, outs):
    found = []
    for keep, turn, dy, grow, dw, width, matrix, (dy_out, dmix_out, dfeat_out) in zip(
        keeps, pointwise, dys, grows, dws, widths, (None, fold), outs[0:2]
    ):
        dy_out[...] = bf(dy)
        dmix, dres = block_backward(keep, turn, dy, grow)
        dmix_out[...] = dmix
        dfeat = feature_cotangent(dmix, dres, dw, width, flags_ref, matrix)
        dfeat_out[...] = dfeat
        found.append(dfeat)
    send_edges(*found, *widths, *outs[2], flags_ref[2] > 0)


def weight_terms(air, sea, widths):
    grads = []
    for model in (air, sea):
        normed, hid, residual, dpre, dres = model[0:5]
        grads.append(dot_nt(bf(normed[...]), dpre[...]))
        grads.append(dot_nt(dres[...], hid[...]))
    wa, ws = widths
    dfeat_a, dfeat_s = bf(air[7][...]), bf(sea[7][...])
    air_stack, sea_stack = air[8], sea[8]
    span = dfeat_s.shape[1]
    blank = jnp.zeros((64, 64), F32)
    for i in range(3):
        part = dot_nt(dfeat_s, sea_stack[:, i * ws : i * ws + span])
        grads.append(jnp.concatenate([part, blank], axis=1))
    span = dfeat_a.shape[1]
    nine = jnp.concatenate([air_stack[:, i * wa : i * wa + span] for i in range(3)], axis=0)
    parts = [dot_nt(dfeat_a, nine), dot_nt(air[2][...], air[5][...]), dot_nt(sea[2][...], sea[5][...])]
    rest = jnp.concatenate(parts + [jnp.zeros((64, 256 - sum(x.shape[1] for x in parts)), F32)], axis=1)
    columns = []
    for model, width in ((air, wa), (sea, ws)):
        dmix = model[6][...]
        columns += depthwise_terms([rolled(dmix, width, by) for by in (1, 0, -1)], model[9][...].astype(F32), width)
    lanes = iota((64, 256), 1)
    for t, column in enumerate(columns):
        rest = rest + jnp.where(lanes == 208 + t, column, 0.0)
    grads.append(rest)
    return grads


def fetch(pairs, sems):
    copies = [pltpu.make_async_copy(src, dst, sems.at[i]) for i, (src, dst) in enumerate(pairs)]
    for copy in copies:
        copy.start()
    for copy in copies:
        copy.wait()


def pack_kernel(flags_ref, *refs):
    sources, outs, held, sems = refs[:8], refs[8:13], refs[13:21], refs[21]
    fetch(list(zip(sources, held)), sems)
    counts_ref, air_ref, sea_ref, flux_ref, ac_ref, sc_ref, ssh_ref, ash_ref = held
    mine, near, far, at_a, at_b = outs
    a = load_rows(air_ref)
    o = load_rows(sea_ref)
    flux = load_rows(flux_ref)
    place = iota((8, LANE), 0) * LANE + iota((8, LANE), 1)
    used = jnp.concatenate([jnp.where(place < counts_ref[0:1, k : k + 1], 1.0, 0.0) for k in range(5)], axis=0)
    ac, sc = ac_ref[...], sc_ref[...]
    wair, wsea = ash_ref[...] * used, ssh_ref[...] * used
    wair_hi, wsea_hi = rounded(wair), rounded(wsea)
    kinds = [
        (ac >> 7).astype(F32), (ac & 127).astype(F32), (sc >> 7).astype(F32), (sc & 127).astype(F32),
        wair_hi, wair - wair_hi, wsea_hi, wsea - wsea_hi,
    ]
    line = lambda x, k: jnp.concatenate([x[8 * k + h : 8 * k + h + 1] for h in range(8)], axis=1)
    air_hi, air_lo, sea_hi, sea_lo, wah, wal, wsh, wsl = [[line(x, k) for k in range(5)] for x in kinds]
    raw = jnp.concatenate([flux, jnp.zeros_like(flux)], axis=0)
    raw = jnp.where(iota((8, 1), 0) == SURFACE, o[0:1], raw)
    heads = []
    for d, off in enumerate(OFFS):
        k, m = 2 + off, 2 - off
        local = [air_hi[k], air_lo[k], sea_hi[m], sea_lo[m], wsh[m], wsl[m], wah[m], wal[m]]
        mine[8 * d : 8 * d + 8] = jnp.concatenate(local, axis=0)
        stat = [sea_hi[k], sea_lo[k], air_hi[m], air_lo[m], wah[k], wal[k], wsh[k], wsl[k]]
        heads.append(jnp.concatenate([raw] + stat, axis=0))
    mine[40:56] = heads[2]
    first, second = sides(heads[4], heads[0], flags_ref[3] > 0)
    at_a[...] = bf(first)
    at_b[...] = bf(second)
    edge = 2 * air_ref.shape[2]
    up = jnp.concatenate([heads[3], band_rows(o, a[:, -edge:])], axis=0)
    dn = jnp.concatenate([heads[1], band_rows(o, a[:, :edge])], axis=0)
    beside, other = sides(up, dn, flags_ref[2] > 0)
    near[...] = bf(beside)
    far[...] = bf(other)


def band_rows(o, a_edge):
    blank = jnp.zeros((8, o.shape[1] - a_edge.shape[1]), F32)
    tail = jnp.concatenate([a_edge, blank], axis=1)
    return jnp.concatenate([o, tail, jnp.zeros_like(tail)], axis=0)


FORMS = {}
FORM_ROWS = 0
for _name, _parts, _rows, _columns in (
    ("aef", 3, 64, 48), ("sef", 3, 64, 192), ("aex", 1, 256, 64), ("sex", 1, 256, 64),
    ("aco", 1, 64, 256), ("sco", 1, 64, 256), ("ade", 1, 16, 64), ("sde", 1, 48, 64),
    ("adw", 1, 64, 9), ("sdw", 1, 64, 9),
):
    FORMS[_name] = (FORM_ROWS, _parts, _rows, _columns)
    FORM_ROWS += _parts * _rows


def forms(ref, *names):
    found = []
    for name in names:
        start, parts, rows, columns = FORMS[name]
        pieces = [ref[start + rows * i : start + rows * (i + 1), 0:columns] for i in range(parts)]
        if name in ("adw", "sdw"):
            pieces = [piece.astype(F32) for piece in pieces]
        found.append(pieces if parts > 1 else pieces[0])
    return found


def prepare_kernel(*refs):
    sources, out, held, sems = refs[:8], refs[8], refs[9:17], refs[17]
    fetch(list(zip(sources, held)), sems)
    aenc, senc, aex_t, sex_t, aco, sco, sde, small = [ref[...] for ref in held]

    def put(name, value, part=0):
        start, _, rows, columns = FORMS[name]
        out[start + rows * part : start + rows * (part + 1), 0:columns] = bf(value)

    kinds = aenc.shape[1] // 9
    for name, weights, padded in (("aef", aenc, 16), ("sef", senc, 64)):
        column = iota((1, 3 * padded), 1)
        kind = column % padded
        if name == "aef":
            last = kind == kinds - 1 + SURFACE
            kind = jnp.where(kind < kinds - 1, kind, jnp.where(last, kinds - 1, -(1 << 20)))
        else:
            kind = jnp.where(kind < senc.shape[1] // 9, kind, -(1 << 20))
        for i in range(3):
            wanted = (3 * i + column // padded) * (weights.shape[1] // 9) + kind
            put(name, dot(weights, bf(jnp.where(iota((weights.shape[1], 1), 0) == wanted, 1.0, 0.0))), i)
    turn = lambda x: x.astype(F32).T
    for name, value in (("aco", aco), ("sco", sco), ("sde", sde), ("aex", turn(aex_t)), ("sex", turn(sex_t))):
        put(name, value)
    put("ade", small[0:16])
    put("adw", turn(small[16:32])[:, 0:9])
    put("sdw", turn(small[32:48])[:, 0:9])


def couple_kernel(flags_ref, mine, near, far, at_a, at_b, _, lists_out, cpl_out):
    up, dn = sides(near[0:16, :].astype(F32), far[0:16, :].astype(F32), flags_ref[2] > 0)
    up2, dn2 = sides(at_a[...].astype(F32), at_b[...].astype(F32), flags_ref[3] > 0)
    heads = [up2, up, mine[40:56], dn, dn2]
    lists = []
    for d, head in enumerate(heads):
        local = mine[8 * d : 8 * d + 8]
        stat = head[8:16]
        lists.append(
            jnp.concatenate([stat[0:2], local[0:2], stat[2:4], local[2:4], stat[4:8], local[4:8]], axis=0)
        )
    lists_out[...] = bf(jnp.concatenate(lists, axis=0))
    cpl = couple([full_paths(rows, True) for rows in lists], [to_table(head[0:CHANNELS]) for head in heads])
    cpl_out[...] = bf(jnp.concatenate([cpl, jnp.zeros_like(cpl)], axis=0))


def couple_again_kernel(place, lists_ref, own, near, at_a, at_b, a_ref, o_ref, cpl_out, near_out, far_out):
    cpl = couple(own_paths(lists_ref, True), tables_around(place, own, near, at_a, at_b))
    cpl_out[...] = bf(jnp.concatenate([cpl, jnp.zeros_like(cpl)], axis=0))
    a, o = a_ref[...], o_ref[...]
    edge = 2 * LANE
    blank = jnp.zeros((8, o.shape[1] - edge), F32)
    for out, rows in zip((near_out, far_out), sides(a[:, -edge:], a[:, :edge], place[2] > 0)):
        out[0:16, :] = bf(jnp.concatenate([cpl, jnp.concatenate([rows, blank], axis=1)], axis=0))
        out[16:64, :] = bf(o)


def model_inputs(a, o, cpl, bands, cpls):
    edge = 2 * LANE
    rows = iota((8, 1), 0)

    def joined(state_a, state_o, coupled, part):
        air = jnp.where(rows == SURFACE, coupled, 0.0)
        air = air if part is None else air[:, part]
        sea = jnp.where(rows < SURFACE, coupled, 0.0)
        return (
            jnp.concatenate([state_a, air], axis=0),
            jnp.concatenate([state_o, sea, jnp.zeros_like(sea)], axis=0),
        )

    below = joined(bands[0][48:56, :edge], bands[0][0:48], cpls[0], slice(-edge, None))
    above = joined(bands[1][48:56, :edge], bands[1][0:48], cpls[1], slice(0, edge))
    own = joined(a, o, cpl, None)
    return (
        jnp.concatenate([below[0], own[0], above[0]], axis=1),
        jnp.concatenate([below[1], own[1], above[1]], axis=1),
    )


def wet_rows(wet_ref):
    wet = wet_ref[...].astype(F32)
    return jnp.concatenate([wet[r : r + 1] for r in range(wet.shape[0])], axis=1)


def put_table(out, raw):
    out[...] = bf(jnp.concatenate([to_table(raw), jnp.zeros((8, LANE), F32)], axis=0))


def forward_kernel(
    flags_ref, air_ref, o_ref, cpl_ref, band_near, band_far, cpl_near, cpl_far, wet_ref, partner_ref,
    weights_ref, a_out, o_out, table_out, air_stack_out, sea_stack_out, air_feat_out, sea_feat_out,
):
    aef, sef, adw, aex, aco, ade, sdw, sex, sco, sde = forms(
        weights_ref, "aef", "sef", "adw", "aex", "aco", "ade", "sdw", "sex", "sco", "sde"
    )
    wa, ws = LANE, wet_ref.shape[1]
    odd = flags_ref[2] > 0
    a, o = load_rows(air_ref), load_rows(o_ref)
    fold = fold_matrix(partner_ref)
    above, below = sides(band_near[...].astype(F32)[16:80], band_far[...].astype(F32)[16:80], odd)
    cpl_up, cpl_dn = sides(cpl_near[...].astype(F32)[0:8], cpl_far[...].astype(F32)[0:8], odd)
    cpl = cpl_ref[...].astype(F32)[0:8]
    xa, xs = model_inputs(a, o, cpl, (below, above), (cpl_dn, cpl_up))
    air_stack, air_feat = features_of(xa, aef, wa, flags_ref, None)
    sea_stack, sea_feat = features_of(xs, sef, ws, flags_ref, fold)
    air_stack_out[...] = air_stack
    sea_stack_out[...] = sea_stack
    air_feat_out[...] = bf(air_feat)
    sea_feat_out[...] = bf(sea_feat)
    y_air = block_forward(mix(air_feat, adw, wa)[0], air_feat[:, wa:-wa], aex[...], aco[...], ade[...])
    y_sea = block_forward(mix(sea_feat, sdw, ws)[0], sea_feat[:, ws:-ws], sex[...], sco[...], sde[...])
    a = a + y_air[0:8]
    o = o + wet_rows(wet_ref) * y_sea
    a_out[...] = a
    o_out[...] = o
    put_table(table_out, jnp.concatenate([y_air[8:12], o[0:1]], axis=0))


def last_kernel(
    flags_ref, a_ref, o_ref, cpl_ref, band_near, band_far, wet_ref, partner_ref,
    acot_ref, ocot_ref, weights_ref,
    air_stack_out, sea_stack_out, air_feat_out, sea_feat_out,
    na, ia, ha, la, ra, ns, is_, hs, ls, rs, pa, ea, ps, es,
    dya, dma, dfa, dys, dms, dfs, near, far,
):
    aef, sef, adw, aex, aco, ade, sdw, sex, sco, sde = forms(
        weights_ref, "aef", "sef", "adw", "aex", "aco", "ade", "sdw", "sex", "sco", "sde"
    )
    wa, ws = LANE, wet_ref.shape[1]
    odd = flags_ref[2] > 0
    a, o = a_ref[...], o_ref[...]
    fold = fold_matrix(partner_ref)
    up, dn = sides(band_near[...].astype(F32), band_far[...].astype(F32), odd)
    below, above = [jnp.concatenate([band[16:64], band[8:16]], axis=0) for band in (dn, up)]
    cpl = cpl_ref[...].astype(F32)[0:8]
    xa, xs = model_inputs(a, o, cpl, (below, above), (dn[0:8], up[0:8]))
    air_stack, air_feat = features_of(xa, aef, wa, flags_ref, None)
    sea_stack, sea_feat = features_of(xs, sef, ws, flags_ref, fold)
    air_stack_out[...] = air_stack
    sea_stack_out[...] = sea_stack
    air_feat_out[...] = bf(air_feat)
    sea_feat_out[...] = bf(sea_feat)
    keeps = ((na, ia, ha, la, ra), (ns, is_, hs, ls, rs))
    block_replay(mix(air_feat, adw, wa)[0], air_feat[:, wa:-wa], aex[...], aco[...], keeps[0])
    block_replay(mix(sea_feat, sdw, ws)[0], sea_feat[:, ws:-ws], sex[...], sco[...], keeps[1])
    wet = wet_rows(wet_ref)
    acot = load_rows(acot_ref)
    pointwise = ((aex, aco, ade), (sex, sco, sde))
    backward_of(
        flags_ref, keeps, pointwise, (jnp.concatenate([acot, jnp.zeros_like(acot)], axis=0), wet * load_rows(ocot_ref)),
        ((pa, ea), (ps, es)), (adw, sdw), (wa, ws), fold, ((dya, dma, dfa), (dys, dms, dfs), (near, far)),
    )


def replay_kernel(
    air_feat_ref, sea_feat_ref, weights_ref, na, ia, ha, la, ra, ns, is_, hs, ls, rs,
):
    adw, aex, aco, sdw, sex, sco = forms(weights_ref, "adw", "aex", "aco", "sdw", "sex", "sco")
    for feat_ref, dw, ex, co, keep in (
        (air_feat_ref, adw, aex, aco, (na, ia, ha, la, ra)),
        (sea_feat_ref, sdw, sex, sco, (ns, is_, hs, ls, rs)),
    ):
        feat = feat_ref[...].astype(F32)
        width = (feat.shape[1] - na.shape[1]) // 2
        block_replay(mix(feat, dw, width)[0], feat[:, width:-width], ex[...], co[...], keep)


def first_kernel(
    place, lists_ref, own, t_near, at_a, at_b, acot_ref, ocot_ref, wet_ref, partner_ref,
    na, ia, ha, la, ra, ns, is_, hs, ls, rs, weights_ref,
    air_stack, sea_stack, air_feat, sea_feat, later,
    ocot_out, dfa, dfs, near, far, grads_out,
    pa, ea, ps, es, dya, dma, dys, dms,
):
    adw, aex, aco, ade, sdw, sex, sco, sde = forms(
        weights_ref, "adw", "aex", "aco", "ade", "sdw", "sex", "sco", "sde"
    )
    wa, ws = LANE, wet_ref.shape[1]
    fold = fold_matrix(partner_ref)
    tables = tables_around(place, own, t_near, at_a, at_b)
    at_air, at_sea = regrid(own_paths(lists_ref, False), tables, False)
    ocot = ocot_ref[...]
    ocot = jnp.where(iota((ocot.shape[0], 1), 0) == 0, ocot + at_sea, ocot)
    ocot_out[...] = ocot
    flux_rows = jnp.concatenate([at_air, jnp.zeros_like(at_air)], axis=0)
    backward_of(
        place, ((na, ia, ha, la, ra), (ns, is_, hs, ls, rs)), ((aex, aco, ade), (sex, sco, sde)),
        (jnp.concatenate([acot_ref[...], flux_rows], axis=0), wet_rows(wet_ref) * ocot),
        ((pa, ea), (ps, es)), (adw, sdw), (wa, ws), fold, ((dya, dma, dfa), (dys, dms, dfs), (near, far)),
    )
    air = (na, ha, ra, pa, ea, dya, dma, dfa, air_stack, air_feat)
    sea = (ns, hs, rs, ps, es, dys, dms, dfs, sea_stack, sea_feat)
    for p, grad in enumerate(weight_terms(air, sea, (wa, ws))):
        total = bf(later[:, 256 * p : 256 * p + 256] + grad)
        for q in range(4):
            for l in range(2):
                row = 16 * (16 * q + 2 * p + l)
                grads_out[row : row + 16, :] = total[16 * q : 16 * q + 16, LANE * l : LANE * (l + 1)]


def last_grads_kernel(*refs):
    air, sea, (a_ref, o_ref, wet_ref, weights_ref), (out, a_out, o_out, done) = refs[0:10], refs[10:20], refs[20:24], refs[24:]
    done[...] = jnp.zeros_like(done)
    widths = LANE, wet_ref.shape[1]
    out[...] = jnp.concatenate(weight_terms(air, sea, widths), axis=1)
    ade, sde = forms(weights_ref, "ade", "sde")
    store_rows(a_out, a_ref[...] + dot(ade, air[2][...])[0:8])
    store_rows(o_out, o_ref[...] + wet_rows(wet_ref) * dot(sde, sea[2][...]))


def input_kernel(
    flags_ref, dfa_ref, dfs_ref, from_near, from_far, acot_ref, ocot_ref, partner_ref, weights_ref, *refs,
):
    acot_out, ocot_out, table_out = refs[-3:]
    aef, sef = forms(weights_ref, "aef", "sef")
    wa, ws = LANE, partner_ref.shape[1]
    fold = fold_matrix(partner_ref)
    up, dn = sides(from_near[...].astype(F32), from_far[...].astype(F32), flags_ref[2] > 0)
    dfa, dfs = dfa_ref[...], dfs_ref[...]
    middle = jnp.zeros((64, dfa.shape[1] - 4 * wa), F32)
    dfa = dfa + jnp.concatenate([dn[:, : 2 * wa], middle, up[:, : 2 * wa]], axis=1)
    dfs = dfs + jnp.concatenate([dn[:, 2 * wa :], up[:, 2 * wa :]], axis=1)
    dxa = input_cotangent(dfa, aef, wa, flags_ref, None)
    dxs = input_cotangent(dfs, sef, ws, flags_ref, fold)
    if len(acot_ref.shape) == 3:
        acot_out[...] = load_rows(acot_ref) + dxa[0:8]
        ocot_out[...] = load_rows(ocot_ref) + dxs[0:48]
    else:
        store_rows(acot_out, acot_ref[...] + dxa[0:8])
        ocot_out[...] = ocot_ref[...] + dxs[0:48]
    put_table(table_out, jnp.concatenate([dxs[48:52], dxa[12:13]], axis=0))


def total_kernel(terms_ref, _, out):
    total = terms_ref[0].astype(F32)
    for i in range(1, terms_ref.shape[0]):
        total = total + terms_ref[i].astype(F32)
    total = bf(total)
    for i in range(out.shape[0]):
        out[i] = total


def final_kernel(flags_ref, lists_ref, own, near, at_a, at_b, ocot_ref, sea_out, flux_out):
    tables = tables_around(flags_ref, own, near, at_a, at_b)
    at_air, at_sea = regrid(own_paths(lists_ref, False), tables, False)
    ocot = ocot_ref[...]
    ocot = jnp.where(iota((ocot.shape[0], 1), 0) == 0, ocot + at_sea, ocot)
    store_rows(sea_out, ocot)
    store_rows(flux_out, at_air)


def unpack_kernel(
    air_scale, sea_scale, sums_ref, acol_ref, scol_ref, ae, adw, aex, aco, ade, se, sdw, sex, sco, sde,
):
    sums = jnp.concatenate([sums_ref[i].astype(F32) for i in range(sums_ref.shape[0])], axis=0)

    def part(p):
        lanes = []
        for l in range(2):
            rows = [16 * (16 * q + 2 * p + l) for q in range(4)]
            lanes.append(jnp.concatenate([sums[row : row + 16] for row in rows], axis=0))
        return jnp.concatenate(lanes, axis=1)

    aex[...] = part(0) * air_scale
    aco[...] = part(1) * air_scale
    sex[...] = part(2) * sea_scale
    sco[...] = part(3) * sea_scale

    def picked(block, wanted, base):
        chosen = bf(jnp.where(iota((256, wanted.shape[1]), 0) + base == wanted, 1.0, 0.0))
        return dot(bf(block), chosen)

    columns = scol_ref[...]
    se[...] = sea_scale * (picked(part(4), columns, 0) + picked(part(5), columns, 256) + picked(part(6), columns, 512))
    rest = part(7)
    ae[...] = air_scale * picked(rest, acol_ref[...], 0)
    across = rest.T
    adw[...] = air_scale * across[208 : 208 + adw.shape[0]]
    sdw[...] = sea_scale * across[217 : 217 + sdw.shape[0]]
    ade[...] = air_scale * across[144 : 144 + ade.shape[0]]
    sde[...] = sea_scale * across[160 : 160 + sde.shape[0]]


VMEM = pl.BlockSpec(memory_space=pltpu.VMEM)


def place():
    position, count = lax.axis_index("tile"), lax.axis_size("tile")
    return [jnp.int32(0) + x for x in (position == 0, position == count - 1, position % 2, position // 2 % 2)]


def placed_kernel(kernel):
    return lambda *refs: kernel(place(), *refs)


def call(kernel, name, outs, args, scratch=(), specs=None, cost=None, limit=VMEM_LIMIT):
    return pl.pallas_call(
        kernel,
        out_shape=[jax.ShapeDtypeStruct(shape, kind) for shape, kind in outs],
        in_specs=specs or [VMEM] * len(args),
        out_specs=[VMEM] * len(outs),
        scratch_shapes=list(scratch),
        compiler_params=pltpu.CompilerParams(vmem_limit_bytes=limit),
        cost_estimate=cost and pl.CostEstimate(flops=int(cost), bytes_accessed=4 << 20, transcendentals=0),
        name=name,
    )(*args)


def chips_beside(at_a, at_b):
    length = lax.axis_size("tile")
    first = [(i, i ^ 2) for i in range(length)]
    second = [(i, j) for i in range(length) for j in [((i + 2) ^ 2) - 2] if 0 <= j < length]
    at_b = lax.ppermute(at_b, "tile", second)
    return lax.ppermute(at_a, "tile", first), at_b


def beside(near, far):
    length = lax.axis_size("tile")
    chip = [(i, i ^ 1) for i in range(length)]
    other = [(i, j) for i in range(length) for j in [((i + 1) ^ 1) - 1] if 0 <= j < length]
    far = lax.ppermute(far, "tile", other)
    return lax.ppermute(near, "tile", chip), far


def to_all(blocks):
    return lax.all_to_all(blocks, "tile", 0, 0)


def around(table):
    length = lax.axis_size("tile")
    near = lax.ppermute(table, "tile", [(i, i ^ 1) for i in range(length)])
    pair = jnp.concatenate([table, near], axis=0)
    return (table, near, *chips_beside(pair, pair))


def body(
    air_state, sea_state, flux_start, air_cells, sea_cells, slot_counts, sea_share, air_share,
    polar_fold_partner, wet_mask, air_cotangent, sea_cotangent,
    air_encoder, air_depthwise, air_expand, air_contract, air_decoder,
    sea_encoder, sea_depthwise, sea_expand, sea_contract, sea_decoder,
):
    devices = lax.axis_size("tile")
    ach, air_rows, air_width = air_state.shape
    och, sea_rows, sea_width = sea_state.shape
    flux = flux_start.shape[0]
    slots = air_cells.shape[2]
    air_sites, sea_sites = air_rows * air_width, sea_rows * sea_width
    partner = polar_fold_partner.reshape(1, sea_width)

    air_columns, sea_columns = [], []
    for t in range(9):
        i, j = divmod(t, 3)
        air_columns += [48 * i + 16 * j + (k if k < ach else ach + SURFACE) for k in range(ach + 1)]
        sea_columns += [256 * i + 64 * j + k for k in range(och + flux)]
    air_columns, sea_columns = np.array([air_columns], np.int32), np.array([sea_columns], np.int32)

    lines = lambda x: x.reshape(-1, LANE)
    sources = (
        slot_counts, air_state, sea_state, flux_start,
        lines(air_cells), lines(sea_cells), lines(sea_share), lines(air_share),
    )
    head = ((16, sea_sites), BF)
    band = ((80, sea_sites), BF)
    mine, near, far, at_a, at_b = call(
        placed_kernel(pack_kernel), "pack",
        [((56, slots), F32), band, band, head, head],
        sources,
        specs=[pl.BlockSpec(memory_space=pltpu.HBM)] * len(sources),
        limit=60 * 1024 * 1024,
        scratch=[pltpu.VMEM(x.shape, x.dtype) for x in sources] + [pltpu.SemaphoreType.DMA((len(sources),))],
    )
    band_near, band_far = beside(near, far)
    at_a, at_b = chips_beside(at_a, at_b)
    rows_of = lambda x, count: jnp.pad(x, ((0, count - x.shape[0]), (0, 0)))
    small = [rows_of(air_decoder, 16), rows_of(air_depthwise.T, 16), rows_of(sea_depthwise.T, 16)]
    sources = (
        air_encoder, sea_encoder, air_expand.T, sea_expand.T, air_contract, sea_contract, sea_decoder,
        jnp.concatenate(small, axis=0),
    )
    (weights,) = call(
        prepare_kernel, "prepare", [((FORM_ROWS, 256), BF)], sources,
        specs=[pl.BlockSpec(memory_space=pltpu.HBM)] * len(sources), limit=60 * 1024 * 1024, cost=3e9,
        scratch=[pltpu.VMEM(x.shape, x.dtype) for x in sources] + [pltpu.SemaphoreType.DMA((len(sources),))],
    )
    lists, cpl = call(
        placed_kernel(couple_kernel), "couple", [((80, slots), BF), head],
        (mine, band_near, band_far, at_a, at_b, weights),
        specs=[VMEM] * 5 + [pl.BlockSpec(memory_space=pltpu.HBM)],
    )
    cpl_near, cpl_far = beside(cpl, cpl)
    stacks = [((48, (air_rows + 4) * air_width), BF), ((192, (sea_rows + 4) * sea_width), BF)]
    feats = [((64, (air_rows + 2) * air_width), BF), ((64, (sea_rows + 2) * sea_width), BF)]
    keeps, grows, backs = [], [], []
    for sites, outputs, (feat, _) in ((air_sites, 16, feats[0]), (sea_sites, och, feats[1])):
        keeps += [((64, sites), F32), ((8, sites), F32), ((256, sites), BF), ((256, sites), BF), ((64, sites), BF)]
        grows += [((256, sites), BF), ((64, sites), BF)]
        backs += [((outputs, sites), BF), ((64, sites), F32), (feat, F32)]
    halo = ((64, 2 * air_width + 2 * sea_width), BF)
    table = ((48, LANE), BF)
    state = ((64, sea_sites), BF)
    a1, o1, own, ast, sst, aft, sft = call(
        placed_kernel(forward_kernel), "forward",
        [((ach, air_sites), F32), ((och, sea_sites), F32), table, *stacks, *feats],
        (air_state, sea_state, cpl, band_near, band_far, cpl_near, cpl_far, wet_mask, partner, weights),
    )
    cpl, near, far = call(
        placed_kernel(couple_again_kernel), "couple_again", [head, state, state], (lists, *around(own), a1, o1)
    )
    band_near, band_far = beside(near, far)
    ast1, sst1, aft1, sft1, *rest = call(
        placed_kernel(last_kernel), "last",
        [*stacks, *feats, *keeps, *grows, *backs, halo, halo],
        (a1, o1, cpl, band_near, band_far, wet_mask, partner, air_cotangent, sea_cotangent,
         weights),
    )
    keep, (pa, ea, ps, es, dya, dma, dfa, dys, dms, dfs, near, far) = rest[:10], rest[10:]
    edge_near, edge_far = beside(near, far)
    gathered = lambda keep, pa, ea, ps, es, dya, dma, dfa, dys, dms, dfs, ast, sst, aft, sft: (
        keep[0], keep[2], keep[4], pa, ea, dya, dma, dfa, ast, aft,
        keep[5], keep[7], keep[9], ps, es, dys, dms, dfs, sst, sft,
    )
    token = ((8, LANE), F32)
    later, air_final, sea_final, done = call(
        last_grads_kernel, "last_grads", [((64, 2048), F32), (air_state.shape, F32), (sea_state.shape, F32), token],
        (*gathered(keep, pa, ea, ps, es, dya, dma, dfa, dys, dms, dfs, ast1, sst1, aft1, sft1),
         a1, o1, wet_mask, weights), cost=3e9,
    )
    acot, ocot, own = call(
        placed_kernel(input_kernel), "inputs", [((ach, air_sites), F32), ((och, sea_sites), F32), table],
        (dfa, dfs, edge_near, edge_far, air_cotangent, sea_cotangent, partner, weights, done),
    )

    keep = call(
        replay_kernel, "replay", keeps, (aft, sft, weights), cost=3e9
    )
    kept = [pltpu.VMEM(shape, kind) for shape, kind in grows + backs[0:2] + backs[3:5]]
    ocot, dfa, dfs, near, far, grads = call(
        placed_kernel(first_kernel), "first",
        [((och, sea_sites), F32), backs[2], backs[5], halo, halo, ((8 * LANE, LANE), BF)],
        (lists, *around(own), acot, ocot, wet_mask, partner, *keep, weights, ast, sst, aft, sft, later),
        scratch=kept,
    )
    edge_near, edge_far = beside(near, far)
    terms = to_all(grads.reshape(devices, -1, LANE))
    air_grad, ocot, own = call(
        placed_kernel(input_kernel), "first_inputs", [(air_state.shape, F32), ((och, sea_sites), F32), table],
        (dfa, dfs, edge_near, edge_far, acot, ocot, partner, weights), cost=5e10,
    )
    tables = around(own)
    (sums,) = call(total_kernel, "total", [(terms.shape, BF)], (terms, tables[2]))
    sums = to_all(sums)
    sea_grad, flux_grad = call(
        placed_kernel(final_kernel), "final", [(sea_state.shape, F32), (flux_start.shape, F32)],
        (lists, *tables, ocot), cost=5e10,
    )
    air_scale = 1.0 / math.sqrt(air_sites * devices)
    sea_scale = 1.0 / math.sqrt(sea_sites * devices)
    flipped = lambda w: (w.shape[1], w.shape[0])
    shapes = [
        air_encoder.shape, flipped(air_depthwise), flipped(air_expand), air_contract.shape, air_decoder.shape,
        sea_encoder.shape, flipped(sea_depthwise), flipped(sea_expand), sea_contract.shape, sea_decoder.shape,
    ]
    ae, dwa, exa, coa, dea, se, dws, exs, cos, des = call(
        lambda *refs: unpack_kernel(air_scale, sea_scale, *refs), "unpack", [(shape, F32) for shape in shapes],
        (sums, air_columns, sea_columns),
    )
    return (
        air_final, sea_final, air_grad, sea_grad, flux_grad,
        ae, dwa.T, exa.T, coa, dea, se, dws.T, exs.T, cos, des,
    )


def solution(mesh):
    rows = P(None, "tile", None)
    blocks = P("tile", None, None)
    placed = (
        (rows,) * 3 + (blocks,) * 2 + (P("tile", None),) + (blocks,) * 2 + (P(), P("tile", None)) + (rows,) * 2 + (P(),) * 10
    )
    return jax.shard_map(
        body, mesh=mesh, in_specs=placed, out_specs=(rows,) * 5 + (P(),) * 10, check_vma=False
    )
```
